128 devices in a mesh: group: 16 (over z, y), cell: 8 (over x, core).
Axes of the slice: x: 4, y: 4, z: 4, core: 2. Of those that a mesh axis runs over, the one named last changes fastest.
Arguments:
- rest_shape: bfloat16 [3, 8192, 512], P(None, ('group', 'cell')), may hold values from -3 to 3
- state_start: float32 [12, 8192], P(None, ('group', 'cell')), may hold values from -3 to 3
- state_pred: float32 [12, 8192], P(None, ('group', 'cell')), may hold values from -3 to 3
- body_mass: float32 [8192], P(('group', 'cell')), may hold values from 0.5 to 4
- pair_body: int32 [786432], P(('group', 'cell')), may hold values from 0 to 63
- pair_vertex: int32 [786432], P(('group', 'cell')), may hold values from 0 to 511
- far_body: int32 [786432], P(('group', 'cell')), may hold values from 0 to 511
- far_vertex: int32 [786432], P(('group', 'cell')), may hold values from 0 to 511
- counts: int32 [128, 128], P(('group', 'cell')), may hold values from 0 to 48, as said below
Outputs:
- state_end: float32 [12, 8192], P(None, ('group', 'cell'))
The draws below stay inside these ranges and needn't reach their ends.
Inputs may be any that keep to these rules, and one draw needn't show every extreme that they name: `counts`: entries of a row vary with the receiving device: a receiver's live slots from each sender lie between one and two eighths of 48 times a level of 1 to 4 drawn for that receiver; at least one entry equals 48.
All inputs are finite; a program needn't handle non-finite values.
Results may differ from the reference program's by a relative error of at most 0.00085.
Values may be sent and summed in bfloat16 or wider, within the bound.
A program may use at most 192 MiB of HBM per device.

```python
import math
import jax
import jax.numpy as jnp
from jax import lax

V = 512
B_DEV = 64
ROWS_DEV = 6144
NEWTON = 2
BODIES = 8192
CAP = 48
ROWS = 786432
N_GROUP = 16
N_CELL = 8


def draw_counts(key, part):
    devices = N_GROUP * N_CELL
    key_level, key_raw, key_place = jax.random.split(jax.random.fold_in(key, 11), 3)
    level = jax.random.randint(key_level, (devices, 1), 1, 5)
    lowest = CAP * level // 8
    highest = CAP * level // 4 + 1
    raw_draw = jax.random.randint(key_raw, (devices, devices), 0, 1 << 20)
    amounts = lowest + raw_draw % (highest - lowest)
    place = jax.random.randint(key_place, (), 0, devices * devices)
    flat = jnp.where(jnp.arange(devices * devices) == place, CAP, amounts.reshape(-1))
    return flat.reshape(devices, devices).astype(jnp.int32)


def place_ends(entries, own_key, least, high):
    spot = [jax.random.randint(jax.random.fold_in(own_key, axis), (), 0, length) for axis, length in enumerate(entries.shape)]
    longest = entries.shape.index(max(entries.shape))
    beside = spot[:longest] + [(spot[longest] + 1) % entries.shape[longest]] + spot[longest + 1:]
    return entries.at[tuple(spot)].set(least).at[tuple(beside)].set(high)


def shard_levels(key, dims, cuts, least, high):
    def one(position, shards_of):
        steps = jax.random.uniform(jax.random.fold_in(jax.random.fold_in(key, 6), position), (shards_of,), jnp.float32, least / len(cuts), high / len(cuts))
        return jnp.repeat(jnp.exp(steps), dims[position] // shards_of).reshape((-1,) + (1,) * (len(dims) - position - 1))

    loudness = one(*cuts[0])
    for cut in cuts[1:]:
        loudness = loudness * one(*cut)
    return loudness


def normal_values(key, extent, scale, reach, cuts=(), kind=jnp.bfloat16):
    factor_of = shard_levels(key, extent, cuts, -0.22, 0.18) if cuts else 1.0
    values = jax.random.normal(key, extent, jnp.float32) * scale * factor_of
    return jnp.minimum(jnp.maximum(values, -reach), reach).astype(kind)


def setup_inputs(seed: int = 0) -> dict:
    keys = jax.random.split(jax.random.key(seed), 10)
    return {
        "rest_shape": normal_values(keys[0], (3, BODIES, V), 0.5, 3.0, ((1, 128),)),
        "state_start": normal_values(keys[1], (12, BODIES), 0.5, 3.0, ((1, 128),), jnp.float32),
        "state_pred": normal_values(keys[2], (12, BODIES), 0.5, 3.0, ((1, 128),), jnp.float32),
        "body_mass": jnp.clip(jnp.exp(math.log(4.0) - 2.0794415 * jax.random.uniform(keys[3], (BODIES,), jnp.float32) ** shard_levels(keys[3], (BODIES,), ((0, 128),), -0.2, 0.2)), 0.5, 4.0),
        "pair_body": place_ends(jax.random.randint(keys[4], (ROWS,), 0, B_DEV), jax.random.fold_in(keys[4], 1), 0, B_DEV - 1).astype(jnp.int32),
        "pair_vertex": place_ends(jax.random.randint(keys[5], (ROWS,), 0, V), jax.random.fold_in(keys[5], 1), 0, V - 1).astype(jnp.int32),
        "far_body": place_ends(jax.random.randint(keys[6], (ROWS,), 0, N_CELL * B_DEV), jax.random.fold_in(keys[6], 1), 0, (N_CELL * B_DEV) - 1).astype(jnp.int32),
        "far_vertex": place_ends(jax.random.randint(keys[7], (ROWS,), 0, V), jax.random.fold_in(keys[7], 1), 0, V - 1).astype(jnp.int32),
        "counts": draw_counts(jax.random.fold_in(keys[9], 71), 0),
    }


KC0 = 40.0
KAPPA = 2.0
HIGH = lax.Precision.HIGHEST

def world_points(state, points):
    return state[0:3] + points[0:1] * state[3:6] + points[1:2] * state[6:9] + points[2:3] * state[9:12]

def inertia_blocks(rest_full, body_mass):
    verts = rest_full.shape[2]
    lever = jnp.concatenate([jnp.ones((1,) + rest_full.shape[1:], jnp.float32), rest_full], 0)
    moment = jnp.einsum('mbv,nbv->bmn', lever, lever, precision=HIGH) / verts
    moment = moment * body_mass[:, None, None]
    identity = jnp.eye(3, dtype=jnp.float32)
    return jnp.einsum('bmn,ik->bmink', moment, identity).reshape(moment.shape[0], 12, 12)

def row_features(near_rest, offset, alive, barrier):
    width = offset.shape[1]
    square = lax.optimization_barrier(jnp.sum(offset * offset, 0))
    inverse = 1.0 / (square + 1.0)
    grad_coef = -2.0 * barrier * inverse * inverse * alive
    weight_one = 2.0 * barrier * inverse * inverse * alive
    root_two = jnp.sqrt(8.0 * barrier * inverse * inverse * inverse * alive)
    lever = jnp.concatenate([jnp.ones((1, width), jnp.float32), near_rest], 0)
    grad_rows = (lever[:, None, :] * (grad_coef * offset)[None]).reshape(12, width)
    moment_rows = (lever[:, None, :] * lever[None, :, :] * weight_one).reshape(16, width)
    vector_rows = (lever[:, None, :] * (root_two * offset)[None]).reshape(12, width)
    outer_rows = (vector_rows[:, None, :] * vector_rows[None, :, :]).reshape(144, width)
    return jnp.concatenate([grad_rows, moment_rows, outer_rows], 0)

def cholesky_blocks(hessian):
    factor = [[None] * 12 for _ in range(12)]
    for col in range(12):
        running = hessian[:, col, col]
        for inner in range(col):
            running = running - factor[col][inner] * factor[col][inner]
        pivot = jnp.sqrt(running)
        factor[col][col] = pivot
        for row in range(col + 1, 12):
            value = hessian[:, row, col]
            for inner in range(col):
                value = value - factor[row][inner] * factor[col][inner]
            factor[row][col] = value / pivot
    return factor

def solve_blocks(factor, gradient):
    forward = []
    for row in range(12):
        running = gradient[:, row]
        for col in range(row):
            running = running - factor[row][col] * forward[col]
        forward.append(running / factor[row][row])
    backward = [None] * 12
    for row in reversed(range(12)):
        running = forward[row]
        for col in range(row + 1, 12):
            running = running - factor[col][row] * backward[col]
        backward[row] = running / factor[row][row]
    return jnp.stack(backward, 1)

def newton_update(state, state_pred, inertia, totals):
    bodies = state.shape[1]
    stiff = jnp.array([0, 0, 0, 1, 1, 1, 1, 1, 1, 1, 1, 1], jnp.float32)
    target = jnp.array([0, 0, 0, 1, 0, 0, 0, 1, 0, 0, 0, 1], jnp.float32)
    identity = jnp.eye(3, dtype=jnp.float32)
    contact_grad = totals[0:12].T
    moments = totals[12:28].T.reshape(bodies, 4, 4)
    outers = totals[28:172].T.reshape(bodies, 12, 12)
    contact_hess = jnp.einsum('bmn,ik->bmink', moments, identity).reshape(bodies, 12, 12) + outers
    offset = (state - state_pred).T
    gradient = jnp.einsum('bkl,bl->bk', inertia, offset, precision=HIGH) + 2.0 * KAPPA * stiff * (state.T - target) + contact_grad
    hessian = inertia + jnp.diag(2.0 * KAPPA * stiff)[None] + contact_hess
    factor = cholesky_blocks(hessian)
    return state - solve_blocks(factor, gradient).T

def reference(rest_shape, state_start, state_pred, body_mass, pair_body, pair_vertex, far_body, far_vertex, counts):
    devices = N_GROUP * N_CELL
    capacity = ROWS_DEV // devices
    barrier = KC0 * B_DEV / ROWS_DEV
    rest_full = rest_shape.astype(jnp.float32)
    inertia = inertia_blocks(rest_full, body_mass)
    order = jnp.arange(ROWS_DEV, dtype=jnp.int32)
    source = order // capacity
    slot = order % capacity
    live_rows = (slot[None, :] < counts[:, source]).astype(jnp.float32)
    group_base = (source // N_CELL * (N_CELL * B_DEV)).astype(jnp.int32)
    far_ids = far_body.reshape(devices, devices, capacity).transpose(1, 0, 2).reshape(devices, ROWS_DEV) + group_base[None, :]
    far_points = far_vertex.reshape(devices, devices, capacity).transpose(1, 0, 2).reshape(devices, ROWS_DEV)
    near_ids = pair_body.reshape(devices, ROWS_DEV)
    near_points = pair_vertex.reshape(devices, ROWS_DEV)
    starts = jnp.arange(devices, dtype=jnp.int32) * B_DEV
    state = state_start
    for newton_step in range(NEWTON):

        def per_device(inputs, state=state):
            first_body, near_body, near_point, far_ids_dev, far_point, alive = inputs
            local_state = lax.dynamic_slice_in_dim(state, first_body, B_DEV, 1)
            local_rest = lax.dynamic_slice_in_dim(rest_full, first_body, B_DEV, 1)
            near_rest = local_rest[:, near_body, near_point]
            near_x = world_points(local_state[:, near_body], near_rest)
            far_x = world_points(state[:, far_ids_dev], rest_full[:, far_ids_dev, far_point])
            features = row_features(near_rest, near_x - far_x, alive, barrier)
            return jax.ops.segment_sum(features.T, near_body, num_segments=B_DEV).T
        totals = lax.map(per_device, (starts, near_ids, near_points, far_ids, far_points, live_rows))
        totals = totals.transpose(1, 0, 2).reshape(172, BODIES)
        state = newton_update(state, state_pred, inertia, totals)
    return state
```

```python
import jax
import jax.numpy as jnp
from jax import lax
from jax.experimental import pallas as pl
from jax.experimental.pallas import tpu as pltpu
from jax.sharding import PartitionSpec as P

NEWTON = 2
KC0 = 40.0
KAPPA = 2.0
MESH = pl.DeviceIdType.MESH
F32 = jnp.float32
BF16 = jnp.bfloat16
I32 = jnp.int32

V = 512
B = 64
ROWS = 6144
CAP = 48
NG = 16
NC = 8
DENSE = (ROWS // 128, 128)
PER_G = ROWS // NG
W_NEAR = 512
W_FAR = 256
NT = (((1,), (1,)), ((), ()))

MN = [(m, n) for m in range(4) for n in range(m, 4)]
IK = [(i, k) for i in range(3) for k in range(i, 3)]


def iota(shape, dim):
    return lax.broadcasted_iota(I32, shape, dim)


def one_hot_vertex(vertex):
    width = vertex.shape[1]
    rows = (iota((V, width), 0) - V // 2).astype(BF16)
    mine = jnp.broadcast_to((vertex - V // 2).astype(BF16), (V, width))
    return jnp.where(rows == mine, jnp.ones((), BF16), jnp.zeros((), BF16))


def pick_bodies(acc, picked, body, blocks):
    for n in range(blocks):
        for bg in range(B // 8):
            mine = body == n * B + bg * 8
            for c in range(3):
                at = n * 3 * B + c * B + bg * 8
                acc[c] = jnp.where(mine, picked[at : at + 8], acc[c])
    return acc


def gather_lanes(row, index):
    return jnp.take_along_axis(
        jnp.broadcast_to(row, index.shape), index, axis=1, mode="promise_in_bounds"
    )


def solve(hess, grad):
    factor = [[None] * 12 for _ in range(12)]
    inv = [None] * 12
    for col in range(12):
        running = hess(col, col)
        for inner in range(col):
            running = running - factor[col][inner] * factor[col][inner]
        inv[col] = 1.0 / jnp.sqrt(running)
        for row in range(col + 1, 12):
            value = hess(row, col)
            for inner in range(col):
                value = value - factor[row][inner] * factor[col][inner]
            factor[row][col] = value * inv[col]
    forward = []
    for row in range(12):
        running = grad[row]
        for col in range(row):
            running = running - factor[row][col] * forward[col]
        forward.append(running * inv[row])
    backward = [None] * 12
    for row in reversed(range(12)):
        running = forward[row]
        for col in range(row + 1, 12):
            running = running - factor[col][row] * backward[col]
        backward[row] = running * inv[row]
    return backward


def kernel(
    rest_ref, state_ref, pred_ref, mass_ref, nb_ref, nv_ref, fb_ref, fv_ref, counts_ref,
    out_ref,
    restg, ksend, krecv, ssend, srecv, xsend, xrecv,
    oh, ohb, acc, keyd, vrow, brow, nbrow, nvrow, fbd, fr, nr, live, p16, q9, feat, tot, inert, xd,
    rest_ss, rest_rs, k_ss, k_rs, s_ss, s_rs, x_ss, x_rs,
):
    g = lax.axis_index("group")
    c = lax.axis_index("cell")
    kc = KC0 * B / ROWS

    def cell_peer(d):
        return lax.rem(c + d, NC)

    def group_peer(d):
        return lax.rem(g + d, NG)

    barrier = pltpu.get_barrier_semaphore()

    @pl.loop(1, NC)
    def _(d):
        pl.semaphore_signal(barrier, inc=1, device_id=(g, cell_peer(d)), device_id_type=MESH)

    @pl.loop(1, NG)
    def _(d):
        pl.semaphore_signal(barrier, inc=1, device_id=(group_peer(d), c), device_id_type=MESH)

    for t in range(3):
        rows = pl.ds(t, NG, stride=3)
        keyd[:, t * 128 : (t + 1) * 128] = fb_ref[rows, :] * V + fv_ref[rows, :]
    ksend[...] = jnp.zeros_like(ksend)
    for s in range(NC):
        ksend[s, :, 0:CAP] = keyd[:, s * CAP : (s + 1) * CAP]
    ssend[...] = jnp.zeros_like(ssend)
    ssend[0, 0:12, :] = jnp.concatenate([state_ref[...], state_ref[...]], axis=1)

    pl.semaphore_wait(barrier, NC - 1 + NG - 1)

    def key_copy(to, slot):
        return pltpu.make_async_remote_copy(
            ksend.at[to], krecv.at[slot], k_ss.at[to], k_rs.at[slot],
            device_id=(g, to), device_id_type=MESH,
        )

    def rest_copy(to, slot):
        return pltpu.make_async_remote_copy(
            rest_ref, restg.at[slot], rest_ss.at[to], rest_rs.at[slot],
            device_id=(g, to), device_id_type=MESH,
        )

    def state_copy(it, to, slot):
        return pltpu.make_async_remote_copy(
            ssend.at[it], srecv.at[it, slot], s_ss.at[it, to], s_rs.at[it, slot],
            device_id=(g, to), device_id_type=MESH,
        )

    def x_copy(it, to, slot):
        return pltpu.make_async_remote_copy(
            xsend.at[it, to], xrecv.at[it, slot], x_ss.at[it, to], x_rs.at[it, slot],
            device_id=(to, c), device_id_type=MESH,
        )

    @pl.loop(1, NC)
    def _(d):
        key_copy(cell_peer(d), c).start()

    @pl.loop(1, NC)
    def _(d):
        rest_copy(cell_peer(d), c).start()

    @pl.loop(1, NC)
    def _(d):
        state_copy(0, cell_peer(d), c).start()

    restg[c] = rest_ref[...]
    krecv[c] = ksend[c]
    srecv[0, c] = ssend[0]

    @pl.loop(0, DENSE[0])
    def _(j):
        lanes = pl.ds(pl.multiple_of(j * 128, 128), 128)
        nvrow[0:1, lanes] = nv_ref[pl.ds(j, 1), :]
        nbrow[0:1, lanes] = nb_ref[pl.ds(j, 1), :]

    p16[...] = jnp.zeros_like(p16)

    @pl.loop(0, ROWS // W_NEAR)
    def _(j):
        lanes = pl.ds(pl.multiple_of(j * W_NEAR, W_NEAR), W_NEAR)
        picked = jnp.dot(
            rest_ref[...], one_hot_vertex(nvrow[0:1, lanes]), preferred_element_type=F32
        )
        body = nbrow[0:1, lanes]
        ohb[:, lanes] = jnp.where(
            iota((B, W_NEAR), 0) == jnp.broadcast_to(body, (B, W_NEAR)), 1.0, 0.0
        ).astype(BF16)
        tile = jnp.broadcast_to(body, (8, W_NEAR)) - iota((8, W_NEAR), 0)
        found = pick_bodies([jnp.zeros((8, W_NEAR), F32)] * 3, picked, tile, 1)
        r = [jnp.sum(f, 0, keepdims=True) for f in found]
        lever = [jnp.ones((1, W_NEAR), F32)] + r
        for f, (m, n) in enumerate(MN):
            p16[f : f + 1, lanes] = lever[m] * lever[n]
        for i in range(3):
            for t in range(W_NEAR // 128):
                nr[i, pl.ds(j * (W_NEAR // 128) + t, 1), :] = r[i][:, t * 128 : (t + 1) * 128]

    row = iota(DENSE, 0) * 128 + iota(DENSE, 1)
    sender = (row * 43691) >> 21
    count = gather_lanes(counts_ref[...], sender)
    live[...] = jnp.where(row - sender * CAP < count, 1.0, 0.0)

    ones = jnp.ones((8, V), BF16)
    body_rest = [rest_ref[i * B : (i + 1) * B, :] for i in range(3)]
    scale = mass_ref[...] * (1.0 / V)
    inert[0:1, :] = mass_ref[...]
    for f, (m, n) in enumerate(MN):
        if n == 0:
            continue
        if m == 0:
            total = lax.dot_general(ones, body_rest[n - 1], NT, preferred_element_type=F32)
        else:
            product = body_rest[m - 1].astype(F32) * body_rest[n - 1].astype(F32)
            high = product.astype(BF16)
            low = (product - high.astype(F32)).astype(BF16)
            total = lax.dot_general(ones, high, NT, preferred_element_type=F32)
            total = total + lax.dot_general(ones, low, NT, preferred_element_type=F32)
        inert[f : f + 1, :] = total[0:1] * scale

    @pl.loop(1, NC)
    def _(d):
        key_copy(c, cell_peer(d)).wait_recv()

    for s in range(NC):
        keyd[:, s * CAP : (s + 1) * CAP] = krecv[s, :, 0:CAP]
    for t in range(3):
        fbd[pl.ds(t, NG, stride=3), :] = keyd[:, t * 128 : (t + 1) * 128] >> 9

    @pl.loop(0, NG)
    def _(j):
        lanes = pl.ds(pl.multiple_of(j * PER_G, 128), PER_G)
        key = keyd[pl.ds(j, 1), :]
        vrow[0:1, lanes] = key & (V - 1)
        brow[0:1, lanes] = key >> 9

    @pl.loop(0, ROWS // W_NEAR)
    def _(j):
        lanes = pl.ds(pl.multiple_of(j * W_NEAR, W_NEAR), W_NEAR)
        oh[:, lanes] = one_hot_vertex(vrow[0:1, lanes])

    acc[...] = jnp.zeros_like(acc)
    x = lax.div(c, 2)
    for step, d in enumerate((0, 1, 3, 2)):
        chip = lax.rem(x + d, NC // 2)
        if step == 0:
            rest_copy(c, c + 1 - 2 * lax.rem(c, 2)).wait_recv()
        else:
            for k in range(2):
                rest_copy(c, chip * 2 + k).wait_recv()

        def look(j, carry, chip=chip):
            lanes = pl.ds(pl.multiple_of(j * W_FAR, W_FAR), W_FAR)
            table = restg[pl.ds(chip * 2, 2)].reshape(2 * 3 * B, V)
            picked = jnp.dot(table, oh[:, lanes], preferred_element_type=F32)
            body = jnp.broadcast_to(brow[0:1, lanes] - chip * 2 * B, (8, W_FAR))
            found = [acc[i * 8 : i * 8 + 8, lanes] for i in range(3)]
            found = pick_bodies(found, picked, body - iota((8, W_FAR), 0), 2)
            for i in range(3):
                acc[i * 8 : i * 8 + 8, lanes] = found[i]
            return carry

        lax.fori_loop(0, ROWS // W_FAR, look, 0, unroll=4)

    @pl.loop(0, DENSE[0])
    def _(j):
        lanes = pl.ds(pl.multiple_of(j * 128, 128), 128)
        for i in range(3):
            fr[i, pl.ds(j, 1), :] = jnp.sum(acc[i * 8 : i * 8 + 8, lanes], 0, keepdims=True)

    state = [state_ref[e : e + 1, :] for e in range(12)]
    for it in range(NEWTON):
        @pl.loop(1, NC)
        def _(d, it=it):
            state_copy(it, c, cell_peer(d)).wait_recv()

        pick = iota((16, 128), 1) < B
        low = fbd[...] & 127
        chip_of = fbd[...] >> 7
        far = [None] * 12
        for chip in range(NC // 2):
            table = jnp.where(pick, srecv[it, 2 * chip], srecv[it, 2 * chip + 1])
            here = chip_of == chip
            for e in range(12):
                value = gather_lanes(table[e : e + 1], low)
                far[e] = value if chip == 0 else jnp.where(here, value, far[e])
        for i in range(3):
            xd[i] = far[i] + fr[0] * far[3 + i] + fr[1] * far[6 + i] + fr[2] * far[9 + i]

        @pl.loop(0, NG)
        def _(j, it=it):
            for i in range(3):
                for t in range(3):
                    at = i * PER_G + t * 128
                    xsend[it, j, :, at : at + 128] = xd[i, pl.ds(j * 3 + t, 1), :]

        @pl.loop(1, NG)
        def _(d, it=it):
            x_copy(it, group_peer(d), g).start()

        xrecv[it, g] = xsend[it, g]

        near_index = nb_ref[...]
        near = [gather_lanes(jnp.concatenate([s, s], axis=1), near_index) for s in state]
        near_x = [
            near[i] + nr[0] * near[3 + i] + nr[1] * near[6 + i] + nr[2] * near[9 + i]
            for i in range(3)
        ]

        @pl.loop(1, NG)
        def _(d, it=it):
            x_copy(it, g, group_peer(d)).wait_recv()

        @pl.loop(0, NG)
        def _(j, it=it):
            for i in range(3):
                for t in range(3):
                    at = i * PER_G + t * 128
                    xd[i, pl.ds(j * 3 + t, 1), :] = xrecv[it, j, :, at : at + 128]

        off = [near_x[i] - xd[i] for i in range(3)]
        w = 1.0 / (off[0] * off[0] + off[1] * off[1] + off[2] * off[2] + 1.0)
        h1 = (2.0 * kc) * w * w * live[...]
        h2 = 4.0 * h1 * w
        for f, (i, k) in enumerate(IK):
            value = h2 * off[i] * off[k]
            q9[f] = value + h1 if i == k else value
        for i in range(3):
            q9[6 + i] = -h1 * off[i]

        def features(j, carry):
            lanes = pl.ds(pl.multiple_of(j * 128, 128), 128)
            lever = p16[:, lanes]
            for f in range(6):
                value = lever * q9[f, pl.ds(j, 1), :]
                high = value.astype(BF16)
                feat[f * 16 : f * 16 + 16, lanes] = high
                feat[128 + f * 16 : 128 + f * 16 + 16, lanes] = (value - high.astype(F32)).astype(
                    BF16
                )
            for f, pair in enumerate(((6, 7), (8, 8))):
                value = jnp.concatenate(
                    [lever[0:8] * q9[q, pl.ds(j, 1), :] for q in pair], axis=0
                )
                high = value.astype(BF16)
                at = 96 + f * 16
                feat[at : at + 16, lanes] = high
                feat[128 + at : 128 + at + 16, lanes] = (value - high.astype(F32)).astype(BF16)
            return carry

        lax.fori_loop(0, DENSE[0], features, 0, unroll=2)
        both = lax.dot_general(feat[...], ohb[...], NT, preferred_element_type=F32)
        tot[...] = both[0:128] + both[128:256]

        def moment(m, n):
            f = MN.index((min(m, n), max(m, n)))
            return inert[f : f + 1, :]

        def hess(a, b):
            (m, i), (n, k) = divmod(a, 3), divmod(b, 3)
            f = IK.index((min(i, k), max(i, k))) * 16 + MN.index((min(m, n), max(m, n)))
            value = tot[f : f + 1, :]
            if i == k:
                value = value + moment(m, n)
            if a == b and m > 0:
                value = value + 2.0 * KAPPA
            return value

        shift = [state[e] - pred_ref[e : e + 1, :] for e in range(12)]
        grad = []
        for e in range(12):
            m, i = divmod(e, 3)
            at = 96 + i * 8 + m
            value = tot[at : at + 1, :]
            for n in range(4):
                value = value + moment(m, n) * shift[3 * n + i]
            if m > 0:
                value = value + 2.0 * KAPPA * (state[e] - (1.0 if m - 1 == i else 0.0))
            grad.append(value)
        step = solve(hess, grad)
        state = [state[e] - step[e] for e in range(12)]
        if it + 1 < NEWTON:
            for e in range(12):
                ssend[it + 1, e : e + 1, :] = jnp.concatenate([state[e], state[e]], axis=1)

            @pl.loop(1, NC)
            def _(d, it=it):
                state_copy(it + 1, cell_peer(d), c).start()

            srecv[it + 1, c] = ssend[it + 1]
        else:
            for e in range(12):
                out_ref[e : e + 1, :] = state[e]

    @pl.loop(1, NC)
    def _(d):
        key_copy(cell_peer(d), c).wait_send()
        rest_copy(cell_peer(d), c).wait_send()
        for it in range(NEWTON):
            state_copy(it, cell_peer(d), c).wait_send()

    @pl.loop(1, NG)
    def _(d):
        for it in range(NEWTON):
            x_copy(it, group_peer(d), g).wait_send()


def on_device(rest, state, pred, mass, pair_body, pair_vertex, far_body, far_vertex, counts):
    dma = pltpu.SemaphoreType.DMA
    vmem = pltpu.VMEM
    return pl.pallas_call(
        kernel,
        out_shape=jax.ShapeDtypeStruct((12, B), F32),
        in_specs=[pl.BlockSpec(memory_space=vmem)] * 9,
        out_specs=pl.BlockSpec(memory_space=vmem),
        scratch_shapes=[
            vmem((NC, 3 * B, V), BF16),
            vmem((NC, NG, 128), I32),
            vmem((NC, NG, 128), I32),
            vmem((NEWTON, 16, 128), F32),
            vmem((NEWTON, NC, 16, 128), F32),
            vmem((NEWTON, NG, 1, 3 * PER_G), F32),
            vmem((NEWTON, NG, 1, 3 * PER_G), F32),
            vmem((V, ROWS), BF16),
            vmem((B, ROWS), BF16),
            vmem((24, ROWS), F32),
            vmem((NG, PER_G), I32),
            vmem((1, ROWS), I32),
            vmem((1, ROWS), I32),
            vmem((1, ROWS), I32),
            vmem((1, ROWS), I32),
            vmem(DENSE, I32),
            vmem((3,) + DENSE, F32),
            vmem((3,) + DENSE, F32),
            vmem(DENSE, F32),
            vmem((16, ROWS), F32),
            vmem((9,) + DENSE, F32),
            vmem((256, ROWS), BF16),
            vmem((128, B), F32),
            vmem((16, B), F32),
            vmem((3,) + DENSE, F32),
            dma((NC,)),
            dma((NC,)),
            dma((NC,)),
            dma((NC,)),
            dma((NEWTON, NC)),
            dma((NEWTON, NC)),
            dma((NEWTON, NG)),
            dma((NEWTON, NG)),
        ],
        compiler_params=pltpu.CompilerParams(
            collective_id=0, has_side_effects=True, vmem_limit_bytes=48 * 2**20
        ),
    )(
        rest.reshape(3 * B, V),
        state,
        pred,
        mass.reshape(1, B),
        pair_body.reshape(DENSE),
        pair_vertex.reshape(DENSE),
        far_body.reshape(DENSE),
        far_vertex.reshape(DENSE),
        counts,
    )


def solution(mesh):
    both = ("group", "cell")
    return jax.shard_map(
        on_device,
        mesh=mesh,
        in_specs=(
            P(None, both, None),
            P(None, both),
            P(None, both),
            P(both),
            P(both),
            P(both),
            P(both),
            P(both),
            P(both, None),
        ),
        out_specs=P(None, both),
        check_vma=False,
    )
```

```python
import jax
import jax.numpy as jnp
from jax import lax
from jax.experimental import pallas as pl
from jax.experimental.pallas import tpu as pltpu
from jax.sharding import PartitionSpec as P

NEWTON = 2
KC0 = 40.0
KAPPA = 2.0
MESH = pl.DeviceIdType.MESH
F32 = jnp.float32
BF16 = jnp.bfloat16
I32 = jnp.int32

V = 512
B = 64
ROWS = 6144
CAP = 48
NG = 16
NC = 8
DENSE = (ROWS // 128, 128)
PER_G = ROWS // NG
W = 256
FEATURES = 88
NT = (((1,), (1,)), ((), ()))

MN = [(m, n) for m in range(4) for n in range(m, 4)]
IK = [(i, k) for i in range(3) for k in range(i, 3)]


def iota(shape, dim):
    return lax.broadcasted_iota(I32, shape, dim)


def one_hot_vertex(vertex):
    width = vertex.shape[1]
    rows = (iota((V, width), 0) - V // 2).astype(BF16)
    mine = jnp.broadcast_to((vertex - V // 2).astype(BF16), (V, width))
    return jnp.where(rows == mine, jnp.ones((), BF16), jnp.zeros((), BF16))


def pair_of(ref, j):
    return jnp.concatenate([ref[pl.ds(2 * j, 1), :], ref[pl.ds(2 * j + 1, 1), :]], axis=1)


def pick_bodies(acc, picked, body, blocks):
    for n in range(blocks):
        for bg in range(B // 8):
            mine = body == n * B + bg * 8
            for c in range(3):
                at = n * 3 * B + c * B + bg * 8
                acc[c] = jnp.where(mine, picked[at : at + 8], acc[c])
    return acc


def gather_lanes(row, index):
    return jnp.take_along_axis(
        jnp.broadcast_to(row, index.shape), index, axis=1, mode="promise_in_bounds"
    )


def solve(hess, grad):
    factor = [[None] * 12 for _ in range(12)]
    inv = [None] * 12
    for col in range(12):
        running = hess(col, col)
        for inner in range(col):
            running = running - factor[col][inner] * factor[col][inner]
        inv[col] = 1.0 / jnp.sqrt(running)
        for row in range(col + 1, 12):
            value = hess(row, col)
            for inner in range(col):
                value = value - factor[row][inner] * factor[col][inner]
            factor[row][col] = value * inv[col]
    forward = []
    for row in range(12):
        running = grad[row]
        for col in range(row):
            running = running - factor[row][col] * forward[col]
        forward.append(running * inv[row])
    backward = [None] * 12
    for row in reversed(range(12)):
        running = forward[row]
        for col in range(row + 1, 12):
            running = running - factor[col][row] * backward[col]
        backward[row] = running * inv[row]
    return backward


def kernel(
    rest_in, state_in, pred_in, mass_in, nb_in, nv_in, fb_in, fv_in, counts_in,
    out_ref,
    state_ref, pred_ref, mass_ref, nb_ref, nv_ref, fb_ref, fv_ref, counts_ref,
    restg, ksend, krecv, ssend, srecv, xsend, xrecv,
    oh, ohb, acc, keyd, fkd, fr, nr, live, p16, q8, q2, feat, tot, inert, xd,
    in_s, rest_ss, rest_rs, k_ss, k_rs, s_ss, s_rs, x_ss, x_rs,
):
    g = lax.axis_index("group")
    c = lax.axis_index("cell")
    kc = KC0 * B / ROWS

    def cell_peer(d):
        return lax.rem(c + d, NC)

    def group_peer(d):
        return lax.rem(g + d, NG)

    to_vmem = [
        pltpu.make_async_copy(source, target, in_s.at[n])
        for n, (source, target) in enumerate(
            (
                (fb_in, fb_ref), (fv_in, fv_ref), (state_in, state_ref), (nv_in, nv_ref),
                (nb_in, nb_ref), (rest_in, restg.at[c]), (counts_in, counts_ref),
                (mass_in, mass_ref), (pred_in, pred_ref),
            )
        )
    ]
    for copy in to_vmem:
        copy.start()

    barrier = pltpu.get_barrier_semaphore()

    @pl.loop(1, NC)
    def _(d):
        pl.semaphore_signal(barrier, inc=1, device_id=(g, cell_peer(d)), device_id_type=MESH)

    @pl.loop(1, NG)
    def _(d):
        pl.semaphore_signal(barrier, inc=1, device_id=(group_peer(d), c), device_id_type=MESH)

    for copy in to_vmem[:3]:
        copy.wait()

    for t in range(3):
        rows = pl.ds(t, NG, stride=3)
        keyd[:, t * 128 : (t + 1) * 128] = fb_ref[rows, :] * V + fv_ref[rows, :]
    ksend[...] = jnp.zeros_like(ksend)
    for s in range(NC):
        ksend[s, :, 0:CAP] = keyd[:, s * CAP : (s + 1) * CAP]
    ssend[...] = jnp.zeros_like(ssend)
    ssend[0, 0:12, :] = jnp.concatenate([state_ref[...], state_ref[...]], axis=1)

    pl.semaphore_wait(barrier, NC - 1 + NG - 1)

    def key_copy(to, slot):
        return pltpu.make_async_remote_copy(
            ksend.at[to], krecv.at[slot], k_ss.at[to], k_rs.at[slot],
            device_id=(g, to), device_id_type=MESH,
        )

    x, core = lax.div(c, 2), lax.rem(c, 2)
    chips = [lax.rem(x + d, NC // 2) for d in range(NC // 2)]
    here, right, opposite, left = chips
    other = here * 2 + 1 - core
    halves = (pl.ds(0, 3 * B // 2), pl.ds(3 * B // 2, 3 * B // 2))

    def rest_copy(n, slot, to, half=None):
        ref = restg.at[slot] if half is None else restg.at[slot, halves[half]]
        return pltpu.make_async_remote_copy(
            ref, ref, rest_ss.at[n], rest_rs.at[slot, half or 0],
            device_id=(g, to), device_id_type=MESH,
        )

    rest_sends = [
        pltpu.make_async_remote_copy(
            rest_in, restg.at[c], rest_ss.at[n], rest_rs.at[c, 0],
            device_id=(g, to), device_id_type=MESH,
        )
        for n, to in enumerate((other, right * 2 + core, left * 2 + core))
    ]

    def hand_on(n, slot, to, half=None):
        copy = rest_copy(n, slot, to, half)
        copy.start()
        rest_sends.append(copy)

    def state_copy(it, to, slot):
        return pltpu.make_async_remote_copy(
            ssend.at[it], srecv.at[it, slot], s_ss.at[it, to], s_rs.at[it, slot],
            device_id=(g, to), device_id_type=MESH,
        )

    def x_copy(it, to, slot):
        return pltpu.make_async_remote_copy(
            xsend.at[it, to], xrecv.at[it, slot], x_ss.at[it, to], x_rs.at[it, slot],
            device_id=(to, c), device_id_type=MESH,
        )

    @pl.loop(1, NC)
    def _(d):
        key_copy(cell_peer(d), c).start()

    for copy in rest_sends:
        copy.start()

    @pl.loop(1, NC)
    def _(d):
        state_copy(0, cell_peer(d), c).start()

    krecv[c] = ksend[c]
    srecv[0, c] = ssend[0]
    for copy in to_vmem[3:]:
        copy.wait()

    p16[...] = jnp.zeros_like(p16)

    def near_lookup(j, carry):
        lanes = pl.ds(pl.multiple_of(j * W, W), W)
        picked = jnp.dot(restg[c], one_hot_vertex(pair_of(nv_ref, j)), preferred_element_type=F32)
        body = pair_of(nb_ref, j)
        ohb[:, lanes] = jnp.where(
            iota((B, W), 0) == jnp.broadcast_to(body, (B, W)), 1.0, 0.0
        ).astype(BF16)
        tile = jnp.broadcast_to(body, (8, W)) - iota((8, W), 0)
        found = pick_bodies([jnp.zeros((8, W), F32)] * 3, picked, tile, 1)
        r = [jnp.sum(f, 0, keepdims=True) for f in found]
        lever = [jnp.ones((1, W), F32)] + r
        for f, (m, n) in enumerate(MN):
            p16[f : f + 1, lanes] = lever[m] * lever[n]
        for i in range(3):
            for t in range(2):
                nr[i, pl.ds(2 * j + t, 1), :] = r[i][:, t * 128 : (t + 1) * 128]
        return carry

    lax.fori_loop(0, ROWS // W, near_lookup, 0, unroll=4)

    row = iota(DENSE, 0) * 128 + iota(DENSE, 1)
    sender = (row * 43691) >> 21
    count = gather_lanes(counts_ref[...], sender)
    live[...] = jnp.where(row - sender * CAP < count, 1.0, 0.0)

    ones = jnp.ones((8, V), BF16)
    body_rest = [restg[c, i * B : (i + 1) * B, :] for i in range(3)]
    scale = mass_ref[...] * (1.0 / V)
    inert[0:1, :] = mass_ref[...]
    for f, (m, n) in enumerate(MN):
        if n == 0:
            continue
        if m == 0:
            total = lax.dot_general(ones, body_rest[n - 1], NT, preferred_element_type=F32)
        else:
            product = body_rest[m - 1].astype(F32) * body_rest[n - 1].astype(F32)
            high = product.astype(BF16)
            low = (product - high.astype(F32)).astype(BF16)
            total = lax.dot_general(ones, high, NT, preferred_element_type=F32)
            total = total + lax.dot_general(ones, low, NT, preferred_element_type=F32)
        inert[f : f + 1, :] = total[0:1] * scale

    @pl.loop(1, NC)
    def _(d):
        key_copy(c, cell_peer(d)).wait_recv()

    for s in range(NC):
        keyd[:, s * CAP : (s + 1) * CAP] = krecv[s, :, 0:CAP]
    for t in range(3):
        fkd[pl.ds(t, NG, stride=3), :] = keyd[:, t * 128 : (t + 1) * 128]

    def look(where, first, last, start, stop):
        def step(j, carry):
            lanes = pl.ds(pl.multiple_of(j * W, W), W)
            key = pair_of(fkd, j)
            if first:
                hot = one_hot_vertex(key & (V - 1))
                oh[:, lanes] = hot
                found = [jnp.zeros((8, W), F32)] * 3
            else:
                hot = oh[:, lanes]
                found = [acc[i * 8 : i * 8 + 8, lanes] for i in range(3)]
            body = jnp.broadcast_to(key >> 9, (8, W)) - iota((8, W), 0)
            for chip in where:
                table = restg[pl.ds(chip * 2, 2)].reshape(2 * 3 * B, V)
                picked = jnp.dot(table, hot, preferred_element_type=F32)
                found = pick_bodies(found, picked, body - chip * (2 * B), 2)
            for i in range(3):
                if last:
                    r = jnp.sum(found[i], 0, keepdims=True)
                    for t in range(2):
                        fr[i, pl.ds(2 * j + t, 1), :] = r[:, t * 128 : (t + 1) * 128]
                else:
                    acc[i * 8 : i * 8 + 8, lanes] = found[i]
            return carry

        lax.fori_loop(start, stop, step, 0, unroll=4)

    chunks = ROWS // W
    rest_copy(0, other, other).wait_recv()
    look((here,), True, False, 0, chunks // 2)
    for n, (chip, half, to) in enumerate(((left, 0, right), (right, 1, left))):
        slot = chip * 2 + core
        rest_copy(0, slot, other).wait_recv()
        hand_on(3 + 2 * n, slot, to * 2 + core, half)
        hand_on(4 + 2 * n, slot, other)
    look((here,), True, False, chunks // 2, chunks)
    for chip in (left, right):
        rest_copy(0, chip * 2 + 1 - core, other).wait_recv()
    look((left, right), False, False, 0, chunks // 2)
    for half in range(2):
        slot = opposite * 2 + core
        rest_copy(0, slot, other, half).wait_recv()
        hand_on(7 + half, slot, other, half)
    look((left, right), False, False, chunks // 2, chunks)
    for half in range(2):
        rest_copy(0, opposite * 2 + 1 - core, other, half).wait_recv()
    look((opposite,), False, True, 0, chunks)

    state = [state_ref[e : e + 1, :] for e in range(12)]
    for it in range(NEWTON):
        @pl.loop(1, NC)
        def _(d, it=it):
            state_copy(it, c, cell_peer(d)).wait_recv()

        pick = iota((16, 128), 1) < B
        low = (fkd[...] >> 9) & 127
        chip_of = fkd[...] >> 16
        far = [None] * 12
        for chip in range(NC // 2):
            table = jnp.where(pick, srecv[it, 2 * chip], srecv[it, 2 * chip + 1])
            mine = chip_of == chip
            for e in range(12):
                value = gather_lanes(table[e : e + 1], low)
                far[e] = value if chip == 0 else jnp.where(mine, value, far[e])
        for i in range(3):
            xd[i] = far[i] + fr[0] * far[3 + i] + fr[1] * far[6 + i] + fr[2] * far[9 + i]

        for j in range(NG):
            for i in range(3):
                for t in range(3):
                    at = i * PER_G + t * 128
                    xsend[it, j, :, at : at + 128] = xd[i, j * 3 + t : j * 3 + t + 1, :]

        @pl.loop(1, NG)
        def _(d, it=it):
            x_copy(it, group_peer(d), g).start()

        xrecv[it, g] = xsend[it, g]

        near_index = nb_ref[...]
        near = [gather_lanes(jnp.concatenate([s, s], axis=1), near_index) for s in state]
        near_x = [
            near[i] + nr[0] * near[3 + i] + nr[1] * near[6 + i] + nr[2] * near[9 + i]
            for i in range(3)
        ]

        @pl.loop(1, NG)
        def _(d, it=it):
            x_copy(it, g, group_peer(d)).wait_recv()

        for j in range(NG):
            for i in range(3):
                for t in range(3):
                    at = i * PER_G + t * 128
                    xd[i, j * 3 + t : j * 3 + t + 1, :] = xrecv[it, j, :, at : at + 128]

        off = [near_x[i] - xd[i] for i in range(3)]
        w = 1.0 / (off[0] * off[0] + off[1] * off[1] + off[2] * off[2] + 1.0)
        h1 = (2.0 * kc) * w * w * live[...]
        h2 = 4.0 * h1 * w
        for f, (i, k) in enumerate(IK):
            value = h2 * off[i] * off[k]
            q8[pl.ds(f, DENSE[0], stride=8), :] = value + h1 if i == k else value
        for i in range(2):
            q8[pl.ds(6 + i, DENSE[0], stride=8), :] = -h1 * off[i]
        q2[...] = -h1 * off[2]

        def features(j, carry):
            lanes = pl.ds(pl.multiple_of(j * 128, 128), 128)
            terms = q8[pl.ds(pl.multiple_of(j * 8, 8), 8), :]
            values = [terms * p16[f : f + 1, lanes] for f in range(10)]
            values.append(p16[0:8, lanes] * q2[pl.ds(j, 1), :])
            high = [value.astype(BF16) for value in values]
            low = [(v - h.astype(F32)).astype(BF16) for v, h in zip(values, high)]
            feat[:, lanes] = jnp.concatenate(high + low, axis=0)
            return carry

        lax.fori_loop(0, DENSE[0], features, 0, unroll=4)
        both = lax.dot_general(feat[...], ohb[...], NT, preferred_element_type=F32)
        tot[...] = both[0:FEATURES] + both[FEATURES : 2 * FEATURES]

        def moment(m, n):
            f = MN.index((min(m, n), max(m, n)))
            return inert[f : f + 1, :]

        def hess(a, b):
            (m, i), (n, k) = divmod(a, 3), divmod(b, 3)
            f = IK.index((min(i, k), max(i, k))) + MN.index((min(m, n), max(m, n))) * 8
            value = tot[f : f + 1, :]
            if i == k:
                value = value + moment(m, n)
            if a == b and m > 0:
                value = value + 2.0 * KAPPA
            return value

        shift = [state[e] - pred_ref[e : e + 1, :] for e in range(12)]
        grad = []
        for e in range(12):
            m, i = divmod(e, 3)
            at = m * 8 + 6 + i if i < 2 else 80 + m
            value = tot[at : at + 1, :]
            for n in range(4):
                value = value + moment(m, n) * shift[3 * n + i]
            if m > 0:
                value = value + 2.0 * KAPPA * (state[e] - (1.0 if m - 1 == i else 0.0))
            grad.append(value)
        step = solve(hess, grad)
        state = [state[e] - step[e] for e in range(12)]
        if it + 1 < NEWTON:
            for e in range(12):
                ssend[it + 1, e : e + 1, :] = jnp.concatenate([state[e], state[e]], axis=1)

            @pl.loop(1, NC)
            def _(d, it=it):
                state_copy(it + 1, cell_peer(d), c).start()

            srecv[it + 1, c] = ssend[it + 1]
        else:
            for e in range(12):
                out_ref[e : e + 1, :] = state[e]

    for copy in rest_sends:
        copy.wait_send()

    @pl.loop(1, NC)
    def _(d):
        key_copy(cell_peer(d), c).wait_send()
        for it in range(NEWTON):
            state_copy(it, cell_peer(d), c).wait_send()

    @pl.loop(1, NG)
    def _(d):
        for it in range(NEWTON):
            x_copy(it, group_peer(d), g).wait_send()


def on_device(rest, state, pred, mass, pair_body, pair_vertex, far_body, far_vertex, counts):
    dma = pltpu.SemaphoreType.DMA
    vmem = pltpu.VMEM
    return pl.pallas_call(
        kernel,
        out_shape=jax.ShapeDtypeStruct((12, B), F32),
        in_specs=[pl.BlockSpec(memory_space=pltpu.HBM)] * 9,
        out_specs=pl.BlockSpec(memory_space=vmem),
        scratch_shapes=[
            vmem((12, B), F32),
            vmem((12, B), F32),
            vmem((1, B), F32),
            vmem(DENSE, I32),
            vmem(DENSE, I32),
            vmem(DENSE, I32),
            vmem(DENSE, I32),
            vmem((1, 128), I32),
            vmem((NC, 3 * B, V), BF16),
            vmem((NC, NG, 128), I32),
            vmem((NC, NG, 128), I32),
            vmem((NEWTON, 16, 128), F32),
            vmem((NEWTON, NC, 16, 128), F32),
            vmem((NEWTON, NG, 1, 3 * PER_G), F32),
            vmem((NEWTON, NG, 1, 3 * PER_G), F32),
            vmem((V, ROWS), BF16),
            vmem((B, ROWS), BF16),
            vmem((24, ROWS), F32),
            vmem((NG, PER_G), I32),
            vmem(DENSE, I32),
            vmem((3,) + DENSE, F32),
            vmem((3,) + DENSE, F32),
            vmem(DENSE, F32),
            vmem((16, ROWS), F32),
            vmem((8 * DENSE[0], 128), F32),
            vmem(DENSE, F32),
            vmem((2 * FEATURES, ROWS), BF16),
            vmem((FEATURES, B), F32),
            vmem((16, B), F32),
            vmem((3,) + DENSE, F32),
            dma((9,)),
            dma((9,)),
            dma((NC, 2)),
            dma((NC,)),
            dma((NC,)),
            dma((NEWTON, NC)),
            dma((NEWTON, NC)),
            dma((NEWTON, NG)),
            dma((NEWTON, NG)),
        ],
        compiler_params=pltpu.CompilerParams(
            collective_id=0, has_side_effects=True, vmem_limit_bytes=60 * 2**20
        ),
    )(
        rest.reshape(3 * B, V),
        state,
        pred,
        mass.reshape(1, B),
        pair_body.reshape(DENSE),
        pair_vertex.reshape(DENSE),
        far_body.reshape(DENSE),
        far_vertex.reshape(DENSE),
        counts,
    )


def solution(mesh):
    both = ("group", "cell")
    return jax.shard_map(
        on_device,
        mesh=mesh,
        in_specs=(
            P(None, both, None),
            P(None, both),
            P(None, both),
            P(both),
            P(both),
            P(both),
            P(both),
            P(both),
            P(both, None),
        ),
        out_specs=P(None, both),
        check_vma=False,
    )
```

```python
import jax
import jax.numpy as jnp
from jax import lax
from jax.experimental import pallas as pl
from jax.experimental.pallas import tpu as pltpu
from jax.sharding import PartitionSpec as P

NEWTON = 2
KC0 = 40.0
KAPPA = 2.0
MESH = pl.DeviceIdType.MESH
F32 = jnp.float32
BF16 = jnp.bfloat16
I32 = jnp.int32

V = 512
B = 64
ROWS = 6144
CAP = 48
NG = 16
NC = 8
DENSE = (ROWS // 128, 128)
PER_G = ROWS // NG
W = 256
NEAREST = sorted(
    ((z, y) for z in range(4) for y in range(4)),
    key=lambda d: min(d[0], 4 - d[0]) + min(d[1], 4 - d[1]),
)
PART = 8
FEATURES = 88
NT = (((1,), (1,)), ((), ()))

MN = [(m, n) for m in range(4) for n in range(m, 4)]
IK = [(i, k) for i in range(3) for k in range(i, 3)]


def iota(shape, dim):
    return lax.broadcasted_iota(I32, shape, dim)


def one_hot_vertex(vertex):
    width = vertex.shape[1]
    rows = (iota((V, width), 0) - V // 2).astype(BF16)
    mine = jnp.broadcast_to((vertex - V // 2).astype(BF16), (V, width))
    return jnp.where(rows == mine, jnp.ones((), BF16), jnp.zeros((), BF16))


def pair_of(ref, j):
    return jnp.concatenate([ref[pl.ds(2 * j, 1), :], ref[pl.ds(2 * j + 1, 1), :]], axis=1)


def pick_bodies(acc, picked, body, blocks):
    for n in range(blocks):
        for bg in range(B // 8):
            mine = body == n * B + bg * 8
            for c in range(3):
                at = n * 3 * B + c * B + bg * 8
                acc[c] = jnp.where(mine, picked[at : at + 8], acc[c])
    return acc


def gather_lanes(row, index):
    return jnp.take_along_axis(
        jnp.broadcast_to(row, index.shape), index, axis=1, mode="promise_in_bounds"
    )


def solve(hess, grad):
    factor = [[None] * 12 for _ in range(12)]
    inv = [None] * 12
    for col in range(12):
        running = hess(col, col)
        for inner in range(col):
            running = running - factor[col][inner] * factor[col][inner]
        inv[col] = 1.0 / jnp.sqrt(running)
        for row in range(col + 1, 12):
            value = hess(row, col)
            for inner in range(col):
                value = value - factor[row][inner] * factor[col][inner]
            factor[row][col] = value * inv[col]
    forward = []
    for row in range(12):
        running = grad[row]
        for col in range(row):
            running = running - factor[row][col] * forward[col]
        forward.append(running * inv[row])
    backward = [None] * 12
    for row in reversed(range(12)):
        running = forward[row]
        for col in range(row + 1, 12):
            running = running - factor[col][row] * backward[col]
        backward[row] = running * inv[row]
    return backward


def kernel(
    rest_in, state_in, pred_in, mass_in, nb_in, nv_in, fb_in, fv_in, counts_in,
    out_ref,
    state_ref, pred_ref, mass_ref, nb_ref, nv_ref, fb_ref, fv_ref, counts_ref,
    restg, ksend, krecv, ssend, srecv, xsend, xrecv,
    oh, ohb, acc, keyd, fkd, fr, nr, nb, nv, live, p16, q8, q2, feat, tot, inert, xd,
    in_s, rest_ss, rest_rs, k_ss, k_rs, s_ss, s_rs, x_ss, x_rs,
):
    g = lax.axis_index("group")
    c = lax.axis_index("cell")
    kc = KC0 * B / ROWS

    def cell_peer(d):
        return lax.rem(c + d, NC)

    z, y = lax.div(g, 4), lax.rem(g, 4)
    groups = [lax.rem(z + dz, 4) * 4 + lax.rem(y + dy, 4) for dz, dy in NEAREST]

    def group_peer(d):
        return lax.rem(g + d, NG)

    to_vmem = [
        pltpu.make_async_copy(source, target, in_s.at[n])
        for n, (source, target) in enumerate(
            (
                (fb_in, fb_ref), (fv_in, fv_ref), (state_in, state_ref), (nv_in, nv_ref),
                (nb_in, nb_ref), (rest_in, restg.at[c]), (counts_in, counts_ref),
                (mass_in, mass_ref), (pred_in, pred_ref),
            )
        )
    ]
    for copy in to_vmem:
        copy.start()

    barrier = pltpu.get_barrier_semaphore()

    @pl.loop(1, NC)
    def _(d):
        pl.semaphore_signal(barrier, inc=1, device_id=(g, cell_peer(d)), device_id_type=MESH)

    @pl.loop(1, NG)
    def _(d):
        pl.semaphore_signal(barrier, inc=1, device_id=(group_peer(d), c), device_id_type=MESH)

    for copy in to_vmem[:3]:
        copy.wait()

    for t in range(3):
        rows = pl.ds(t, NG, stride=3)
        keyd[:, t * 128 : (t + 1) * 128] = fb_ref[rows, :] * V + fv_ref[rows, :]
    ksend[...] = jnp.zeros_like(ksend)
    for s in range(NC):
        ksend[s, :, 0:CAP] = keyd[:, s * CAP : (s + 1) * CAP]
    ssend[...] = jnp.zeros_like(ssend)
    ssend[0, 0:12, :] = jnp.concatenate([state_ref[...], state_ref[...]], axis=1)

    pl.semaphore_wait(barrier, NC - 1 + NG - 1)

    def key_copy(to, slot):
        return pltpu.make_async_remote_copy(
            ksend.at[to], krecv.at[slot], k_ss.at[to], k_rs.at[slot],
            device_id=(g, to), device_id_type=MESH,
        )

    x, core = lax.div(c, 2), lax.rem(c, 2)
    chips = [lax.rem(x + d, NC // 2) for d in range(NC // 2)]
    here, right, opposite, left = chips
    other = here * 2 + 1 - core
    halves = (pl.ds(0, 3 * B // 2), pl.ds(3 * B // 2, 3 * B // 2))

    def rest_copy(n, slot, to, half=None):
        ref = restg.at[slot] if half is None else restg.at[slot, halves[half]]
        return pltpu.make_async_remote_copy(
            ref, ref, rest_ss.at[n], rest_rs.at[slot, half or 0],
            device_id=(g, to), device_id_type=MESH,
        )

    rest_sends = [
        pltpu.make_async_remote_copy(
            rest_in, restg.at[c], rest_ss.at[n], rest_rs.at[c, 0],
            device_id=(g, to), device_id_type=MESH,
        )
        for n, to in enumerate((other, right * 2 + core, left * 2 + core))
    ]

    def hand_on(n, slot, to, half=None):
        copy = rest_copy(n, slot, to, half)
        copy.start()
        rest_sends.append(copy)

    def state_copy(it, to, slot):
        return pltpu.make_async_remote_copy(
            ssend.at[it], srecv.at[it, slot], s_ss.at[it, to], s_rs.at[it, slot],
            device_id=(g, to), device_id_type=MESH,
        )

    def x_copy(it, to, slot):
        return pltpu.make_async_remote_copy(
            xsend.at[it, to], xrecv.at[it, slot], x_ss.at[it, to], x_rs.at[it, slot],
            device_id=(to, c), device_id_type=MESH,
        )

    @pl.loop(1, NC)
    def _(d):
        key_copy(cell_peer(d), c).start()

    for copy in rest_sends:
        copy.start()

    @pl.loop(1, NC)
    def _(d):
        state_copy(0, cell_peer(d), c).start()

    krecv[c] = ksend[c]
    srecv[0, c] = ssend[0]
    for copy in to_vmem[3:]:
        copy.wait()

    row = iota(DENSE, 0) * 128 + iota(DENSE, 1)
    sender = (row * 43691) >> 21
    count = gather_lanes(counts_ref[...], sender)
    xd[0] = jnp.where(row - sender * CAP < count, 1.0, 0.0)

    for q, group in enumerate(groups):
        for t in range(3):
            at = pl.ds(group * 3 + t, 1)
            to = pl.ds(q * 3 + t, 1)
            nb[to, :] = nb_ref[at, :]
            nv[to, :] = nv_ref[at, :]
            live[to, :] = xd[0, at, :]

    p16[...] = jnp.zeros_like(p16)

    def near_lookup(j, carry):
        lanes = pl.ds(pl.multiple_of(j * W, W), W)
        picked = jnp.dot(restg[c], one_hot_vertex(pair_of(nv, j)), preferred_element_type=F32)
        body = pair_of(nb, j)
        ohb[:, lanes] = jnp.where(
            iota((B, W), 0) == jnp.broadcast_to(body, (B, W)), 1.0, 0.0
        ).astype(BF16)
        tile = jnp.broadcast_to(body, (8, W)) - iota((8, W), 0)
        found = pick_bodies([jnp.zeros((8, W), F32)] * 3, picked, tile, 1)
        r = [jnp.sum(f, 0, keepdims=True) for f in found]
        lever = [jnp.ones((1, W), F32)] + r
        for f, (m, n) in enumerate(MN):
            p16[f : f + 1, lanes] = lever[m] * lever[n]
        for i in range(3):
            for t in range(2):
                nr[i, pl.ds(2 * j + t, 1), :] = r[i][:, t * 128 : (t + 1) * 128]
        return carry

    lax.fori_loop(0, ROWS // W, near_lookup, 0, unroll=4)

    ones = jnp.ones((8, V), BF16)
    body_rest = [restg[c, i * B : (i + 1) * B, :] for i in range(3)]
    scale = mass_ref[...] * (1.0 / V)
    inert[0:1, :] = mass_ref[...]
    for f, (m, n) in enumerate(MN):
        if n == 0:
            continue
        if m == 0:
            total = lax.dot_general(ones, body_rest[n - 1], NT, preferred_element_type=F32)
        else:
            product = body_rest[m - 1].astype(F32) * body_rest[n - 1].astype(F32)
            high = product.astype(BF16)
            low = (product - high.astype(F32)).astype(BF16)
            total = lax.dot_general(ones, high, NT, preferred_element_type=F32)
            total = total + lax.dot_general(ones, low, NT, preferred_element_type=F32)
        inert[f : f + 1, :] = total[0:1] * scale

    @pl.loop(1, NC)
    def _(d):
        key_copy(c, cell_peer(d)).wait_recv()

    for s in range(NC):
        keyd[:, s * CAP : (s + 1) * CAP] = krecv[s, :, 0:CAP]
    for t in range(3):
        fkd[pl.ds(t, NG, stride=3), :] = keyd[:, t * 128 : (t + 1) * 128]

    def look(where, first, last, start, stop):
        def step(j, carry):
            lanes = pl.ds(pl.multiple_of(j * W, W), W)
            key = pair_of(fkd, j)
            if first:
                hot = one_hot_vertex(key & (V - 1))
                oh[:, lanes] = hot
                found = [jnp.zeros((8, W), F32)] * 3
            else:
                hot = oh[:, lanes]
                found = [acc[i * 8 : i * 8 + 8, lanes] for i in range(3)]
            body = jnp.broadcast_to(key >> 9, (8, W)) - iota((8, W), 0)
            for chip in where:
                table = restg[pl.ds(chip * 2, 2)].reshape(2 * 3 * B, V)
                picked = jnp.dot(table, hot, preferred_element_type=F32)
                found = pick_bodies(found, picked, body - chip * (2 * B), 2)
            for i in range(3):
                if last:
                    r = jnp.sum(found[i], 0, keepdims=True)
                    for t in range(2):
                        fr[i, pl.ds(2 * j + t, 1), :] = r[:, t * 128 : (t + 1) * 128]
                else:
                    acc[i * 8 : i * 8 + 8, lanes] = found[i]
            return carry

        lax.fori_loop(start, stop, step, 0, unroll=4)

    chunks = ROWS // W
    rest_copy(0, other, other).wait_recv()
    look((here,), True, False, 0, chunks // 2)
    for n, (chip, half, to) in enumerate(((left, 0, right), (right, 1, left))):
        slot = chip * 2 + core
        rest_copy(0, slot, other).wait_recv()
        hand_on(3 + 2 * n, slot, to * 2 + core, half)
        hand_on(4 + 2 * n, slot, other)
    look((here,), True, False, chunks // 2, chunks)
    for chip in (left, right):
        rest_copy(0, chip * 2 + 1 - core, other).wait_recv()
    look((left, right), False, False, 0, chunks // 2)
    for half in range(2):
        slot = opposite * 2 + core
        rest_copy(0, slot, other, half).wait_recv()
        hand_on(7 + half, slot, other, half)
    look((left, right), False, False, chunks // 2, chunks)
    for half in range(2):
        rest_copy(0, opposite * 2 + 1 - core, other, half).wait_recv()
    look((opposite,), False, True, 0, chunks)

    state = [state_ref[e : e + 1, :] for e in range(12)]
    for it in range(NEWTON):
        @pl.loop(1, NC)
        def _(d, it=it):
            state_copy(it, c, cell_peer(d)).wait_recv()

        pick = iota((16, 128), 1) < B
        low = (fkd[...] >> 9) & 127
        chip_of = fkd[...] >> 16
        far = [None] * 12
        for chip in range(NC // 2):
            table = jnp.where(pick, srecv[it, 2 * chip], srecv[it, 2 * chip + 1])
            mine = chip_of == chip
            for e in range(12):
                value = gather_lanes(table[e : e + 1], low)
                far[e] = value if chip == 0 else jnp.where(mine, value, far[e])
        for i in range(3):
            xd[i] = far[i] + fr[0] * far[3 + i] + fr[1] * far[6 + i] + fr[2] * far[9 + i]

        for j in range(NG):
            for i in range(3):
                for t in range(3):
                    at = i * PER_G + t * 128
                    xsend[it, j, :, at : at + 128] = xd[i, j * 3 + t : j * 3 + t + 1, :]

        @pl.loop(1, NG)
        def _(d, it=it):
            x_copy(it, group_peer(d), g).start()

        xrecv[it, g] = xsend[it, g]

        near_index = nb[...]
        near = [gather_lanes(jnp.concatenate([s, s], axis=1), near_index) for s in state]
        near_x = [
            near[i] + nr[0] * near[3 + i] + nr[1] * near[6 + i] + nr[2] * near[9 + i]
            for i in range(3)
        ]

        both = jnp.zeros((2 * FEATURES, B), F32)
        for part in range(0, NG, PART):
            for q in range(part, part + PART):
                if q:
                    x_copy(it, g, groups[q]).wait_recv()
                for i in range(3):
                    for t in range(3):
                        at = i * PER_G + t * 128
                        xd[i, q * 3 + t : q * 3 + t + 1, :] = xrecv[it, groups[q], :, at : at + 128]

            rows = slice(part * 3, (part + PART) * 3)
            off = [near_x[i][rows] - xd[i, rows] for i in range(3)]
            w = 1.0 / (off[0] * off[0] + off[1] * off[1] + off[2] * off[2] + 1.0)
            h1 = (2.0 * kc) * w * w * live[rows]
            h2 = 4.0 * h1 * w
            for f, (i, k) in enumerate(IK):
                value = h2 * off[i] * off[k]
                at = pl.ds(rows.start * 8 + f, PART * 3, stride=8)
                q8[at, :] = value + h1 if i == k else value
            for i in range(2):
                q8[pl.ds(rows.start * 8 + 6 + i, PART * 3, stride=8), :] = -h1 * off[i]
            q2[rows, :] = -h1 * off[2]

            for first in range(rows.start, rows.stop, 8):
                for j in range(first, first + 8):
                    lanes = pl.ds(j * 128, 128)
                    terms = q8[j * 8 : j * 8 + 8, :]
                    values = [terms * p16[f : f + 1, lanes] for f in range(10)]
                    values.append(p16[0:8, lanes] * q2[j : j + 1, :])
                    high = [value.astype(BF16) for value in values]
                    low = [(v - h.astype(F32)).astype(BF16) for v, h in zip(values, high)]
                    feat[:, lanes] = jnp.concatenate(high + low, axis=0)
                block = pl.ds(first * 128, 8 * 128)
                both = both + lax.dot_general(
                    feat[:, block], ohb[:, block], NT, preferred_element_type=F32
                )
        tot[...] = both[0:FEATURES] + both[FEATURES : 2 * FEATURES]

        def moment(m, n):
            f = MN.index((min(m, n), max(m, n)))
            return inert[f : f + 1, :]

        def hess(a, b):
            (m, i), (n, k) = divmod(a, 3), divmod(b, 3)
            f = IK.index((min(i, k), max(i, k))) + MN.index((min(m, n), max(m, n))) * 8
            value = tot[f : f + 1, :]
            if i == k:
                value = value + moment(m, n)
            if a == b and m > 0:
                value = value + 2.0 * KAPPA
            return value

        shift = [state[e] - pred_ref[e : e + 1, :] for e in range(12)]
        grad = []
        for e in range(12):
            m, i = divmod(e, 3)
            at = m * 8 + 6 + i if i < 2 else 80 + m
            value = tot[at : at + 1, :]
            for n in range(4):
                value = value + moment(m, n) * shift[3 * n + i]
            if m > 0:
                value = value + 2.0 * KAPPA * (state[e] - (1.0 if m - 1 == i else 0.0))
            grad.append(value)
        step = solve(hess, grad)
        state = [state[e] - step[e] for e in range(12)]
        if it + 1 < NEWTON:
            for e in range(12):
                ssend[it + 1, e : e + 1, :] = jnp.concatenate([state[e], state[e]], axis=1)

            @pl.loop(1, NC)
            def _(d, it=it):
                state_copy(it + 1, cell_peer(d), c).start()

            srecv[it + 1, c] = ssend[it + 1]
        else:
            for e in range(12):
                out_ref[e : e + 1, :] = state[e]

    for copy in rest_sends:
        copy.wait_send()

    @pl.loop(1, NC)
    def _(d):
        key_copy(cell_peer(d), c).wait_send()
        for it in range(NEWTON):
            state_copy(it, cell_peer(d), c).wait_send()

    @pl.loop(1, NG)
    def _(d):
        for it in range(NEWTON):
            x_copy(it, group_peer(d), g).wait_send()


def on_device(rest, state, pred, mass, pair_body, pair_vertex, far_body, far_vertex, counts):
    dma = pltpu.SemaphoreType.DMA
    vmem = pltpu.VMEM
    return pl.pallas_call(
        kernel,
        out_shape=jax.ShapeDtypeStruct((12, B), F32),
        in_specs=[pl.BlockSpec(memory_space=pltpu.HBM)] * 9,
        out_specs=pl.BlockSpec(memory_space=vmem),
        scratch_shapes=[
            vmem((12, B), F32),
            vmem((12, B), F32),
            vmem((1, B), F32),
            vmem(DENSE, I32),
            vmem(DENSE, I32),
            vmem(DENSE, I32),
            vmem(DENSE, I32),
            vmem((1, 128), I32),
            vmem((NC, 3 * B, V), BF16),
            vmem((NC, NG, 128), I32),
            vmem((NC, NG, 128), I32),
            vmem((NEWTON, 16, 128), F32),
            vmem((NEWTON, NC, 16, 128), F32),
            vmem((NEWTON, NG, 1, 3 * PER_G), F32),
            vmem((NEWTON, NG, 1, 3 * PER_G), F32),
            vmem((V, ROWS), BF16),
            vmem((B, ROWS), BF16),
            vmem((24, ROWS), F32),
            vmem((NG, PER_G), I32),
            vmem(DENSE, I32),
            vmem((3,) + DENSE, F32),
            vmem((3,) + DENSE, F32),
            vmem(DENSE, I32),
            vmem(DENSE, I32),
            vmem(DENSE, F32),
            vmem((16, ROWS), F32),
            vmem((8 * DENSE[0], 128), F32),
            vmem(DENSE, F32),
            vmem((2 * FEATURES, ROWS), BF16),
            vmem((FEATURES, B), F32),
            vmem((16, B), F32),
            vmem((3,) + DENSE, F32),
            dma((9,)),
            dma((9,)),
            dma((NC, 2)),
            dma((NC,)),
            dma((NC,)),
            dma((NEWTON, NC)),
            dma((NEWTON, NC)),
            dma((NEWTON, NG)),
            dma((NEWTON, NG)),
        ],
        compiler_params=pltpu.CompilerParams(
            collective_id=0, has_side_effects=True, vmem_limit_bytes=60 * 2**20
        ),
    )(
        rest.reshape(3 * B, V),
        state,
        pred,
        mass.reshape(1, B),
        pair_body.reshape(DENSE),
        pair_vertex.reshape(DENSE),
        far_body.reshape(DENSE),
        far_vertex.reshape(DENSE),
        counts,
    )


def solution(mesh):
    both = ("group", "cell")
    return jax.shard_map(
        on_device,
        mesh=mesh,
        in_specs=(
            P(None, both, None),
            P(None, both),
            P(None, both),
            P(both),
            P(both),
            P(both),
            P(both),
            P(both),
            P(both, None),
        ),
        out_specs=P(None, both),
        check_vma=False,
    )
```

```python
import jax
import jax.numpy as jnp
from jax import lax
from jax.experimental import pallas as pl
from jax.experimental.pallas import tpu as pltpu
from jax.sharding import PartitionSpec as P

NEWTON = 2
KC0 = 40.0
KAPPA = 2.0
MESH = pl.DeviceIdType.MESH
F32 = jnp.float32
BF16 = jnp.bfloat16
I32 = jnp.int32

V = 512
B = 64
ROWS = 6144
CAP = 48
NG = 16
NC = 8
DENSE = (ROWS // 128, 128)
PER_G = ROWS // NG
W = 256
NEAREST = sorted(
    ((z, y) for z in range(4) for y in range(4)),
    key=lambda d: min(d[0], 4 - d[0]) + min(d[1], 4 - d[1]),
)
PART = 8
FEATURES = 88
NT = (((1,), (1,)), ((), ()))

MN = [(m, n) for m in range(4) for n in range(m, 4)]
IK = [(i, k) for i in range(3) for k in range(i, 3)]


def iota(shape, dim):
    return lax.broadcasted_iota(I32, shape, dim)


def one_hot_vertex(vertex):
    width = vertex.shape[1]
    rows = (iota((V, width), 0) - V // 2).astype(BF16)
    mine = jnp.broadcast_to((vertex - V // 2).astype(BF16), (V, width))
    return jnp.where(rows == mine, jnp.ones((), BF16), jnp.zeros((), BF16))


def pair_of(ref, j):
    return jnp.concatenate([ref[pl.ds(2 * j, 1), :], ref[pl.ds(2 * j + 1, 1), :]], axis=1)


def pick_bodies(acc, picked, body, blocks):
    for n in range(blocks):
        for bg in range(B // 8):
            mine = body == n * B + bg * 8
            for c in range(3):
                at = n * 3 * B + c * B + bg * 8
                acc[c] = jnp.where(mine, picked[at : at + 8], acc[c])
    return acc


def gather_lanes(row, index):
    return jnp.take_along_axis(
        jnp.broadcast_to(row, index.shape), index, axis=1, mode="promise_in_bounds"
    )


def solve(hess, grad):
    factor = [[None] * 12 for _ in range(12)]
    inv = [None] * 12
    for col in range(12):
        running = hess(col, col)
        for inner in range(col):
            running = running - factor[col][inner] * factor[col][inner]
        inv[col] = 1.0 / jnp.sqrt(running)
        for row in range(col + 1, 12):
            value = hess(row, col)
            for inner in range(col):
                value = value - factor[row][inner] * factor[col][inner]
            factor[row][col] = value * inv[col]
    forward = []
    for row in range(12):
        running = grad[row]
        for col in range(row):
            running = running - factor[row][col] * forward[col]
        forward.append(running * inv[row])
    backward = [None] * 12
    for row in reversed(range(12)):
        running = forward[row]
        for col in range(row + 1, 12):
            running = running - factor[col][row] * backward[col]
        backward[row] = running * inv[row]
    return backward


def kernel(
    rest_in, state_in, pred_in, mass_in, nb_in, nv_in, fb_in, fv_in, counts_in,
    out_ref,
    state_ref, pred_ref, mass_ref, nb_ref, nv_ref, fb_ref, fv_ref, counts_ref,
    restg, ksend, krecv, ssend, srecv, xsend, xrecv,
    oh, ohb, acc, keyd, fkd, fr, nr, nb, nv, live, p16, q8, q2, feat, tot, inert, xd,
    in_s, rest_ss, rest_rs, k_ss, k_rs, s_ss, s_rs, x_ss, x_rs,
):
    g = lax.axis_index("group")
    c = lax.axis_index("cell")
    kc = KC0 * B / ROWS

    def cell_peer(d):
        return lax.rem(c + d, NC)

    z, y = lax.div(g, 4), lax.rem(g, 4)
    groups = [lax.rem(z + dz, 4) * 4 + lax.rem(y + dy, 4) for dz, dy in NEAREST]

    def group_peer(d):
        return lax.rem(g + d, NG)

    to_vmem = [
        pltpu.make_async_copy(source, target, in_s.at[n])
        for n, (source, target) in enumerate(
            (
                (fb_in, fb_ref), (fv_in, fv_ref), (state_in, state_ref), (nv_in, nv_ref),
                (nb_in, nb_ref), (rest_in, restg.at[c]), (counts_in, counts_ref),
                (mass_in, mass_ref), (pred_in, pred_ref),
            )
        )
    ]
    for copy in to_vmem:
        copy.start()

    barrier = pltpu.get_barrier_semaphore()

    @pl.loop(1, NC)
    def _(d):
        pl.semaphore_signal(barrier, inc=1, device_id=(g, cell_peer(d)), device_id_type=MESH)

    @pl.loop(1, NG)
    def _(d):
        pl.semaphore_signal(barrier, inc=1, device_id=(group_peer(d), c), device_id_type=MESH)

    for copy in to_vmem[:3]:
        copy.wait()

    for t in range(3):
        rows = pl.ds(t, NG, stride=3)
        keyd[:, t * 128 : (t + 1) * 128] = fb_ref[rows, :] * V + fv_ref[rows, :]
    ksend[...] = jnp.zeros_like(ksend)
    for s in range(NC):
        ksend[s, :, 0:CAP] = keyd[:, s * CAP : (s + 1) * CAP]
    ssend[...] = jnp.zeros_like(ssend)
    ssend[0, 0:12, :] = jnp.concatenate([state_ref[...], state_ref[...]], axis=1)

    pl.semaphore_wait(barrier, NC - 1 + NG - 1)

    def key_copy(to, slot):
        return pltpu.make_async_remote_copy(
            ksend.at[to], krecv.at[slot], k_ss.at[to], k_rs.at[slot],
            device_id=(g, to), device_id_type=MESH,
        )

    x, core = lax.div(c, 2), lax.rem(c, 2)
    chips = [lax.rem(x + d, NC // 2) for d in range(NC // 2)]
    here, right, opposite, left = chips
    other = here * 2 + 1 - core
    halves = (pl.ds(0, 3 * B // 2), pl.ds(3 * B // 2, 3 * B // 2))

    def rest_copy(n, slot, to, half=None):
        ref = restg.at[slot] if half is None else restg.at[slot, halves[half]]
        return pltpu.make_async_remote_copy(
            ref, ref, rest_ss.at[n], rest_rs.at[slot, half or 0],
            device_id=(g, to), device_id_type=MESH,
        )

    def first_copy(n, to, half=None):
        source = rest_in if half is None else rest_in.at[halves[half]]
        target = restg.at[c] if half is None else restg.at[c, halves[half]]
        return pltpu.make_async_remote_copy(
            source, target, rest_ss.at[n], rest_rs.at[c, half or 0],
            device_id=(g, to), device_id_type=MESH,
        )

    rest_sends = [
        first_copy(0, right * 2 + core, 0),
        first_copy(1, left * 2 + core, 1),
        first_copy(2, other),
        first_copy(3, right * 2 + core, 1),
        first_copy(4, left * 2 + core, 0),
    ]

    def hand_on(n, slot, to, half=None):
        copy = rest_copy(n, slot, to, half)
        copy.start()
        rest_sends.append(copy)

    def state_copy(it, to, slot):
        return pltpu.make_async_remote_copy(
            ssend.at[it], srecv.at[it, slot], s_ss.at[it, to], s_rs.at[it, slot],
            device_id=(g, to), device_id_type=MESH,
        )

    def x_copy(it, to, slot):
        return pltpu.make_async_remote_copy(
            xsend.at[it, to], xrecv.at[it, slot], x_ss.at[it, to], x_rs.at[it, slot],
            device_id=(to, c), device_id_type=MESH,
        )

    @pl.loop(1, NC)
    def _(d):
        key_copy(cell_peer(d), c).start()

    for copy in rest_sends:
        copy.start()

    @pl.loop(1, NC)
    def _(d):
        state_copy(0, cell_peer(d), c).start()

    krecv[c] = ksend[c]
    srecv[0, c] = ssend[0]
    for copy in to_vmem[3:]:
        copy.wait()

    row = iota(DENSE, 0) * 128 + iota(DENSE, 1)
    sender = (row * 43691) >> 21
    count = gather_lanes(counts_ref[...], sender)
    xd[0] = jnp.where(row - sender * CAP < count, 1.0, 0.0)

    for q, group in enumerate(groups):
        for t in range(3):
            at = pl.ds(group * 3 + t, 1)
            to = pl.ds(q * 3 + t, 1)
            nb[to, :] = nb_ref[at, :]
            nv[to, :] = nv_ref[at, :]
            live[to, :] = xd[0, at, :]

    p16[...] = jnp.zeros_like(p16)

    def near_lookup(j, carry):
        lanes = pl.ds(pl.multiple_of(j * W, W), W)
        picked = jnp.dot(restg[c], one_hot_vertex(pair_of(nv, j)), preferred_element_type=F32)
        body = pair_of(nb, j)
        ohb[:, lanes] = jnp.where(
            iota((B, W), 0) == jnp.broadcast_to(body, (B, W)), 1.0, 0.0
        ).astype(BF16)
        tile = jnp.broadcast_to(body, (8, W)) - iota((8, W), 0)
        found = pick_bodies([jnp.zeros((8, W), F32)] * 3, picked, tile, 1)
        r = [jnp.sum(f, 0, keepdims=True) for f in found]
        lever = [jnp.ones((1, W), F32)] + r
        for f, (m, n) in enumerate(MN):
            p16[f : f + 1, lanes] = lever[m] * lever[n]
        for i in range(3):
            for t in range(2):
                nr[i, pl.ds(2 * j + t, 1), :] = r[i][:, t * 128 : (t + 1) * 128]
        return carry

    lax.fori_loop(0, ROWS // W, near_lookup, 0, unroll=4)

    ones = jnp.ones((8, V), BF16)
    body_rest = [restg[c, i * B : (i + 1) * B, :] for i in range(3)]
    scale = mass_ref[...] * (1.0 / V)
    inert[0:1, :] = mass_ref[...]
    for f, (m, n) in enumerate(MN):
        if n == 0:
            continue
        if m == 0:
            total = lax.dot_general(ones, body_rest[n - 1], NT, preferred_element_type=F32)
        else:
            product = body_rest[m - 1].astype(F32) * body_rest[n - 1].astype(F32)
            high = product.astype(BF16)
            low = (product - high.astype(F32)).astype(BF16)
            total = lax.dot_general(ones, high, NT, preferred_element_type=F32)
            total = total + lax.dot_general(ones, low, NT, preferred_element_type=F32)
        inert[f : f + 1, :] = total[0:1] * scale

    @pl.loop(1, NC)
    def _(d):
        key_copy(c, cell_peer(d)).wait_recv()

    for s in range(NC):
        keyd[:, s * CAP : (s + 1) * CAP] = krecv[s, :, 0:CAP]
    for t in range(3):
        fkd[pl.ds(t, NG, stride=3), :] = keyd[:, t * 128 : (t + 1) * 128]

    def look(where, first, last, start, stop):
        def step(j, carry):
            lanes = pl.ds(pl.multiple_of(j * W, W), W)
            key = pair_of(fkd, j)
            if first:
                hot = one_hot_vertex(key & (V - 1))
                oh[:, lanes] = hot
                found = [jnp.zeros((8, W), F32)] * 3
            else:
                hot = oh[:, lanes]
                found = [acc[i * 8 : i * 8 + 8, lanes] for i in range(3)]
            body = jnp.broadcast_to(key >> 9, (8, W)) - iota((8, W), 0)
            for slot in where:
                picked = jnp.dot(restg[slot], hot, preferred_element_type=F32)
                found = pick_bodies(found, picked, body - slot * B, 1)
            for i in range(3):
                if last:
                    r = jnp.sum(found[i], 0, keepdims=True)
                    for t in range(2):
                        fr[i, pl.ds(2 * j + t, 1), :] = r[:, t * 128 : (t + 1) * 128]
                else:
                    acc[i * 8 : i * 8 + 8, lanes] = found[i]
            return carry

        lax.fori_loop(start, stop, step, 0, unroll=True)

    chunks = ROWS // W
    rest_copy(0, other, other).wait_recv()
    look((c, other), True, False, 0, 10)
    for n, (chip, half, to) in enumerate(((left, 0, right), (right, 1, left))):
        rest_copy(0, chip * 2 + core, other, half).wait_recv()
        hand_on(5 + n, chip * 2 + core, to * 2 + core, half)
    look((c, other), True, False, 10, 24)
    for n, (chip, half) in enumerate(((left, 1), (right, 0))):
        rest_copy(0, chip * 2 + core, other, half).wait_recv()
        hand_on(7 + n, chip * 2 + core, other)
    look((left * 2 + core, right * 2 + core), False, False, 0, 24)
    for half in range(2):
        slot = opposite * 2 + core
        rest_copy(0, slot, other, half).wait_recv()
        hand_on(9 + half, slot, other, half)
    for chip in (left, right):
        rest_copy(0, chip * 2 + 1 - core, other).wait_recv()
    look((left * 2 + 1 - core, right * 2 + 1 - core), False, False, 0, chunks)
    for half in range(2):
        rest_copy(0, opposite * 2 + 1 - core, other, half).wait_recv()
    look((opposite * 2 + core, opposite * 2 + 1 - core), False, True, 0, chunks)

    state = [state_ref[e : e + 1, :] for e in range(12)]
    for it in range(NEWTON):
        @pl.loop(1, NC)
        def _(d, it=it):
            state_copy(it, c, cell_peer(d)).wait_recv()

        pick = iota((16, 128), 1) < B
        low = (fkd[...] >> 9) & 127
        chip_of = fkd[...] >> 16
        far = [None] * 12
        for chip in range(NC // 2):
            table = jnp.where(pick, srecv[it, 2 * chip], srecv[it, 2 * chip + 1])
            mine = chip_of == chip
            for e in range(12):
                value = gather_lanes(table[e : e + 1], low)
                far[e] = value if chip == 0 else jnp.where(mine, value, far[e])
        for i in range(3):
            xd[i] = far[i] + fr[0] * far[3 + i] + fr[1] * far[6 + i] + fr[2] * far[9 + i]

        for j in range(NG):
            for i in range(3):
                for t in range(3):
                    at = i * PER_G + t * 128
                    xsend[it, j, :, at : at + 128] = xd[i, j * 3 + t : j * 3 + t + 1, :]

        @pl.loop(1, NG)
        def _(d, it=it):
            x_copy(it, group_peer(d), g).start()

        xrecv[it, g] = xsend[it, g]

        near_index = nb[...]
        near = [gather_lanes(jnp.concatenate([s, s], axis=1), near_index) for s in state]
        near_x = [
            near[i] + nr[0] * near[3 + i] + nr[1] * near[6 + i] + nr[2] * near[9 + i]
            for i in range(3)
        ]

        both = jnp.zeros((2 * FEATURES, B), F32)
        for part in range(0, NG, PART):
            for q in range(part, part + PART):
                if q:
                    x_copy(it, g, groups[q]).wait_recv()
                for i in range(3):
                    for t in range(3):
                        at = i * PER_G + t * 128
                        xd[i, q * 3 + t : q * 3 + t + 1, :] = xrecv[it, groups[q], :, at : at + 128]

            rows = slice(part * 3, (part + PART) * 3)
            off = [near_x[i][rows] - xd[i, rows] for i in range(3)]
            w = 1.0 / (off[0] * off[0] + off[1] * off[1] + off[2] * off[2] + 1.0)
            h1 = (2.0 * kc) * w * w * live[rows]
            h2 = 4.0 * h1 * w
            for f, (i, k) in enumerate(IK):
                value = h2 * off[i] * off[k]
                at = pl.ds(rows.start * 8 + f, PART * 3, stride=8)
                q8[at, :] = value + h1 if i == k else value
            for i in range(2):
                q8[pl.ds(rows.start * 8 + 6 + i, PART * 3, stride=8), :] = -h1 * off[i]
            q2[rows, :] = -h1 * off[2]

            for first in range(rows.start, rows.stop, 8):
                for j in range(first, first + 8):
                    lanes = pl.ds(j * 128, 128)
                    terms = q8[j * 8 : j * 8 + 8, :]
                    values = [terms * p16[f : f + 1, lanes] for f in range(10)]
                    values.append(p16[0:8, lanes] * q2[j : j + 1, :])
                    high = [value.astype(BF16) for value in values]
                    low = [(v - h.astype(F32)).astype(BF16) for v, h in zip(values, high)]
                    feat[:, lanes] = jnp.concatenate(high + low, axis=0)
                block = pl.ds(first * 128, 8 * 128)
                both = both + lax.dot_general(
                    feat[:, block], ohb[:, block], NT, preferred_element_type=F32
                )
        tot[...] = both[0:FEATURES] + both[FEATURES : 2 * FEATURES]

        def moment(m, n):
            f = MN.index((min(m, n), max(m, n)))
            return inert[f : f + 1, :]

        def hess(a, b):
            (m, i), (n, k) = divmod(a, 3), divmod(b, 3)
            f = IK.index((min(i, k), max(i, k))) + MN.index((min(m, n), max(m, n))) * 8
            value = tot[f : f + 1, :]
            if i == k:
                value = value + moment(m, n)
            if a == b and m > 0:
                value = value + 2.0 * KAPPA
            return value

        shift = [state[e] - pred_ref[e : e + 1, :] for e in range(12)]
        grad = []
        for e in range(12):
            m, i = divmod(e, 3)
            at = m * 8 + 6 + i if i < 2 else 80 + m
            value = tot[at : at + 1, :]
            for n in range(4):
                value = value + moment(m, n) * shift[3 * n + i]
            if m > 0:
                value = value + 2.0 * KAPPA * (state[e] - (1.0 if m - 1 == i else 0.0))
            grad.append(value)
        step = solve(hess, grad)
        state = [state[e] - step[e] for e in range(12)]
        if it + 1 < NEWTON:
            for e in range(12):
                ssend[it + 1, e : e + 1, :] = jnp.concatenate([state[e], state[e]], axis=1)

            @pl.loop(1, NC)
            def _(d, it=it):
                state_copy(it + 1, cell_peer(d), c).start()

            srecv[it + 1, c] = ssend[it + 1]
        else:
            for e in range(12):
                out_ref[e : e + 1, :] = state[e]

    for copy in rest_sends:
        copy.wait_send()

    @pl.loop(1, NC)
    def _(d):
        key_copy(cell_peer(d), c).wait_send()
        for it in range(NEWTON):
            state_copy(it, cell_peer(d), c).wait_send()

    @pl.loop(1, NG)
    def _(d):
        for it in range(NEWTON):
            x_copy(it, group_peer(d), g).wait_send()


def on_device(rest, state, pred, mass, pair_body, pair_vertex, far_body, far_vertex, counts):
    dma = pltpu.SemaphoreType.DMA
    vmem = pltpu.VMEM
    return pl.pallas_call(
        kernel,
        out_shape=jax.ShapeDtypeStruct((12, B), F32),
        in_specs=[pl.BlockSpec(memory_space=pltpu.HBM)] * 9,
        out_specs=pl.BlockSpec(memory_space=vmem),
        scratch_shapes=[
            vmem((12, B), F32),
            vmem((12, B), F32),
            vmem((1, B), F32),
            vmem(DENSE, I32),
            vmem(DENSE, I32),
            vmem(DENSE, I32),
            vmem(DENSE, I32),
            vmem((1, 128), I32),
            vmem((NC, 3 * B, V), BF16),
            vmem((NC, NG, 128), I32),
            vmem((NC, NG, 128), I32),
            vmem((NEWTON, 16, 128), F32),
            vmem((NEWTON, NC, 16, 128), F32),
            vmem((NEWTON, NG, 1, 3 * PER_G), F32),
            vmem((NEWTON, NG, 1, 3 * PER_G), F32),
            vmem((V, ROWS), BF16),
            vmem((B, ROWS), BF16),
            vmem((24, ROWS), F32),
            vmem((NG, PER_G), I32),
            vmem(DENSE, I32),
            vmem((3,) + DENSE, F32),
            vmem((3,) + DENSE, F32),
            vmem(DENSE, I32),
            vmem(DENSE, I32),
            vmem(DENSE, F32),
            vmem((16, ROWS), F32),
            vmem((8 * DENSE[0], 128), F32),
            vmem(DENSE, F32),
            vmem((2 * FEATURES, ROWS), BF16),
            vmem((FEATURES, B), F32),
            vmem((16, B), F32),
            vmem((3,) + DENSE, F32),
            dma((9,)),
            dma((11,)),
            dma((NC, 2)),
            dma((NC,)),
            dma((NC,)),
            dma((NEWTON, NC)),
            dma((NEWTON, NC)),
            dma((NEWTON, NG)),
            dma((NEWTON, NG)),
        ],
        compiler_params=pltpu.CompilerParams(
            collective_id=0, has_side_effects=True, vmem_limit_bytes=60 * 2**20
        ),
    )(
        rest.reshape(3 * B, V),
        state,
        pred,
        mass.reshape(1, B),
        pair_body.reshape(DENSE),
        pair_vertex.reshape(DENSE),
        far_body.reshape(DENSE),
        far_vertex.reshape(DENSE),
        counts,
    )


def solution(mesh):
    both = ("group", "cell")
    return jax.shard_map(
        on_device,
        mesh=mesh,
        in_specs=(
            P(None, both, None),
            P(None, both),
            P(None, both),
            P(both),
            P(both),
            P(both),
            P(both),
            P(both),
            P(both, None),
        ),
        out_specs=P(None, both),
        check_vma=False,
    )
```

```python
import jax
import jax.numpy as jnp
from jax import lax
from jax.experimental import pallas as pl
from jax.experimental.pallas import tpu as pltpu
from jax.sharding import PartitionSpec as P

NEWTON = 2
KC0 = 40.0
KAPPA = 2.0
MESH = pl.DeviceIdType.MESH
F32 = jnp.float32
BF16 = jnp.bfloat16
I32 = jnp.int32

V = 512
B = 64
ROWS = 6144
CAP = 48
NG = 16
NC = 8
DENSE = (ROWS // 128, 128)
PER_G = ROWS // NG
W = 256
NEAREST = sorted(
    ((z, y) for z in range(4) for y in range(4)),
    key=lambda d: min(d[0], 4 - d[0]) + min(d[1], 4 - d[1]),
)
PART = 4
FEATURES = 88
NT = (((1,), (1,)), ((), ()))

MN = [(m, n) for m in range(4) for n in range(m, 4)]
IK = [(i, k) for i in range(3) for k in range(i, 3)]


def iota(shape, dim):
    return lax.broadcasted_iota(I32, shape, dim)


def one_hot_vertex(vertex):
    width = vertex.shape[1]
    rows = (iota((V, width), 0) - V // 2).astype(BF16)
    mine = jnp.broadcast_to((vertex - V // 2).astype(BF16), (V, width))
    return jnp.where(rows == mine, jnp.ones((), BF16), jnp.zeros((), BF16))


def pair_of(ref, j):
    return jnp.concatenate([ref[pl.ds(2 * j, 1), :], ref[pl.ds(2 * j + 1, 1), :]], axis=1)


def pick_bodies(acc, picked, body, blocks):
    for n in range(blocks):
        for bg in range(B // 8):
            mine = body == n * B + bg * 8
            for c in range(3):
                at = n * 3 * B + c * B + bg * 8
                acc[c] = jnp.where(mine, picked[at : at + 8], acc[c])
    return acc


def gather_lanes(row, index):
    return jnp.take_along_axis(
        jnp.broadcast_to(row, index.shape), index, axis=1, mode="promise_in_bounds"
    )


def solve(hess, grad):
    factor = [[None] * 12 for _ in range(12)]
    inv = [None] * 12
    for col in range(12):
        running = hess(col, col)
        for inner in range(col):
            running = running - factor[col][inner] * factor[col][inner]
        inv[col] = 1.0 / jnp.sqrt(running)
        for row in range(col + 1, 12):
            value = hess(row, col)
            for inner in range(col):
                value = value - factor[row][inner] * factor[col][inner]
            factor[row][col] = value * inv[col]
    forward = []
    for row in range(12):
        running = grad[row]
        for col in range(row):
            running = running - factor[row][col] * forward[col]
        forward.append(running * inv[row])
    backward = [None] * 12
    for row in reversed(range(12)):
        running = forward[row]
        for col in range(row + 1, 12):
            running = running - factor[col][row] * backward[col]
        backward[row] = running * inv[row]
    return backward


def kernel(
    rest_in, state_in, pred_in, mass_in, nb_in, nv_in, fb_in, fv_in, counts_in,
    out_ref,
    state_ref, pred_ref, mass_ref, nb_ref, nv_ref, fb_ref, fv_ref, counts_ref,
    restg, ksend, krecv, ssend, srecv, xsend, xrecv,
    oh, ohb, acc, keyd, fkd, fr, nr, nr4, nb, nv, live, p16, q8, q2, feat, tot, inert, xd,
    in_s, rest_ss, rest_rs, k_ss, k_rs, s_ss, s_rs, x_ss, x_rs,
):
    g = lax.axis_index("group")
    c = lax.axis_index("cell")
    kc = KC0 * B / ROWS

    def cell_peer(d):
        return lax.rem(c + d, NC)

    z, y = lax.div(g, 4), lax.rem(g, 4)
    groups = [lax.rem(z + dz, 4) * 4 + lax.rem(y + dy, 4) for dz, dy in NEAREST]

    def group_peer(d):
        return lax.rem(g + d, NG)

    to_vmem = [
        pltpu.make_async_copy(source, target, in_s.at[n])
        for n, (source, target) in enumerate(
            (
                (fb_in, fb_ref), (fv_in, fv_ref), (state_in, state_ref), (nv_in, nv_ref),
                (nb_in, nb_ref), (rest_in, restg.at[c]), (counts_in, counts_ref),
                (mass_in, mass_ref), (pred_in, pred_ref),
            )
        )
    ]
    for copy in to_vmem:
        copy.start()

    barrier = pltpu.get_barrier_semaphore()

    for d in range(1, NC):
        pl.semaphore_signal(barrier, inc=1, device_id=(g, cell_peer(d)), device_id_type=MESH)

    for d in range(1, NG):
        pl.semaphore_signal(barrier, inc=1, device_id=(group_peer(d), c), device_id_type=MESH)

    for copy in to_vmem[:3]:
        copy.wait()

    for t in range(3):
        rows = pl.ds(t, NG, stride=3)
        keyd[:, t * 128 : (t + 1) * 128] = fb_ref[rows, :] * V + fv_ref[rows, :]
    ksend[...] = jnp.zeros_like(ksend)
    for s in range(NC):
        ksend[s, :, 0:CAP] = keyd[:, s * CAP : (s + 1) * CAP]
    ssend[...] = jnp.zeros_like(ssend)
    ssend[0, 0:12, :] = jnp.concatenate([state_ref[...], state_ref[...]], axis=1)

    pl.semaphore_wait(barrier, NC - 1 + NG - 1)

    def key_copy(to, slot):
        return pltpu.make_async_remote_copy(
            ksend.at[to], krecv.at[slot], k_ss.at[to], k_rs.at[slot],
            device_id=(g, to), device_id_type=MESH,
        )

    x, core = lax.div(c, 2), lax.rem(c, 2)
    chips = [lax.rem(x + d, NC // 2) for d in range(NC // 2)]
    here, right, opposite, left = chips
    other = here * 2 + 1 - core
    halves = (pl.ds(0, 3 * B // 2), pl.ds(3 * B // 2, 3 * B // 2))

    def rest_copy(n, slot, to, half=None):
        ref = restg.at[slot] if half is None else restg.at[slot, halves[half]]
        return pltpu.make_async_remote_copy(
            ref, ref, rest_ss.at[n], rest_rs.at[slot, half or 0],
            device_id=(g, to), device_id_type=MESH,
        )

    def first_copy(n, to, half=None):
        source = rest_in if half is None else rest_in.at[halves[half]]
        target = restg.at[c] if half is None else restg.at[c, halves[half]]
        return pltpu.make_async_remote_copy(
            source, target, rest_ss.at[n], rest_rs.at[c, half or 0],
            device_id=(g, to), device_id_type=MESH,
        )

    rest_sends = [
        first_copy(0, right * 2 + core, 0),
        first_copy(1, left * 2 + core, 1),
        first_copy(2, other),
        first_copy(3, right * 2 + core, 1),
        first_copy(4, left * 2 + core, 0),
    ]

    def hand_on(n, slot, to, half=None):
        copy = rest_copy(n, slot, to, half)
        copy.start()
        rest_sends.append(copy)

    def state_copy(it, to, slot):
        return pltpu.make_async_remote_copy(
            ssend.at[it], srecv.at[it, slot], s_ss.at[it, to], s_rs.at[it, slot],
            device_id=(g, to), device_id_type=MESH,
        )

    def x_copy(it, to, slot):
        return pltpu.make_async_remote_copy(
            xsend.at[it, to], xrecv.at[it, slot], x_ss.at[it, to], x_rs.at[it, slot],
            device_id=(to, c), device_id_type=MESH,
        )

    for d in range(1, NC):
        key_copy(cell_peer(d), c).start()

    for copy in rest_sends:
        copy.start()

    for d in range(1, NC):
        state_copy(0, cell_peer(d), c).start()

    krecv[c] = ksend[c]
    srecv[0, c] = ssend[0]
    for copy in to_vmem[3:]:
        copy.wait()

    row = iota(DENSE, 0) * 128 + iota(DENSE, 1)
    sender = (row * 43691) >> 21
    count = gather_lanes(counts_ref[...], sender)
    xd[0] = jnp.where(row - sender * CAP < count, 1.0, 0.0)

    for q, group in enumerate(groups):
        for t in range(3):
            at = pl.ds(group * 3 + t, 1)
            to = pl.ds(q * 3 + t, 1)
            nb[to, :] = nb_ref[at, :]
            nv[to, :] = nv_ref[at, :]
            live[to, :] = xd[0, at, :]

    p16[...] = jnp.zeros_like(p16)

    def near_lookup(j, carry):
        lanes = pl.ds(pl.multiple_of(j * W, W), W)
        picked = jnp.dot(restg[c], one_hot_vertex(pair_of(nv, j)), preferred_element_type=F32)
        body = pair_of(nb, j)
        ohb[:, lanes] = jnp.where(
            iota((B, W), 0) == jnp.broadcast_to(body, (B, W)), 1.0, 0.0
        ).astype(BF16)
        tile = jnp.broadcast_to(body, (8, W)) - iota((8, W), 0)
        found = pick_bodies([jnp.zeros((8, W), F32)] * 3, picked, tile, 1)
        r = [jnp.sum(f, 0, keepdims=True) for f in found]
        lever = [jnp.ones((1, W), F32)] + r
        for f, (m, n) in enumerate(MN):
            p16[f : f + 1, lanes] = lever[m] * lever[n]
        for i in range(3):
            for t in range(2):
                nr[i, pl.ds(2 * j + t, 1), :] = r[i][:, t * 128 : (t + 1) * 128]
        return carry

    lax.fori_loop(0, ROWS // W, near_lookup, 0, unroll=4)

    ones = jnp.ones((8, V), BF16)
    body_rest = [restg[c, i * B : (i + 1) * B, :] for i in range(3)]
    scale = mass_ref[...] * (1.0 / V)
    inert[0:1, :] = mass_ref[...]
    for f, (m, n) in enumerate(MN):
        if n == 0:
            continue
        if m == 0:
            total = lax.dot_general(ones, body_rest[n - 1], NT, preferred_element_type=F32)
        else:
            product = body_rest[m - 1].astype(F32) * body_rest[n - 1].astype(F32)
            high = product.astype(BF16)
            low = (product - high.astype(F32)).astype(BF16)
            total = lax.dot_general(ones, high, NT, preferred_element_type=F32)
            total = total + lax.dot_general(ones, low, NT, preferred_element_type=F32)
        inert[f : f + 1, :] = total[0:1] * scale

    for d in range(1, NC):
        key_copy(c, cell_peer(d)).wait_recv()

    for s in range(NC):
        keyd[:, s * CAP : (s + 1) * CAP] = krecv[s, :, 0:CAP]
    for t in range(3):
        fkd[pl.ds(t, NG, stride=3), :] = keyd[:, t * 128 : (t + 1) * 128]

    def look(where, first, last, start, stop):
        def step(j, carry):
            lanes = pl.ds(pl.multiple_of(j * W, W), W)
            key = pair_of(fkd, j)
            if first:
                hot = one_hot_vertex(key & (V - 1))
                oh[:, lanes] = hot
                found = [jnp.zeros((8, W), F32)] * 3
            else:
                hot = oh[:, lanes]
                found = [acc[i * 8 : i * 8 + 8, lanes] for i in range(3)]
            body = jnp.broadcast_to(key >> 9, (8, W)) - iota((8, W), 0)
            for slot in where:
                picked = jnp.dot(restg[slot], hot, preferred_element_type=F32)
                found = pick_bodies(found, picked, body - slot * B, 1)
            for i in range(3):
                if last:
                    r = jnp.sum(found[i], 0, keepdims=True)
                    for t in range(2):
                        fr[i, pl.ds(2 * j + t, 1), :] = r[:, t * 128 : (t + 1) * 128]
                else:
                    acc[i * 8 : i * 8 + 8, lanes] = found[i]
            return carry

        lax.fori_loop(start, stop, step, 0, unroll=True)

    chunks = ROWS // W
    rest_copy(0, other, other).wait_recv()
    look((c, other), True, False, 0, 10)
    for n, (chip, half, to) in enumerate(((left, 0, right), (right, 1, left))):
        rest_copy(0, chip * 2 + core, other, half).wait_recv()
        hand_on(5 + n, chip * 2 + core, to * 2 + core, half)
    look((c, other), True, False, 10, 24)
    for n, (chip, half) in enumerate(((left, 1), (right, 0))):
        rest_copy(0, chip * 2 + core, other, half).wait_recv()
        hand_on(7 + n, chip * 2 + core, other)
    look((left * 2 + core, right * 2 + core), False, False, 0, 24)
    for half in range(2):
        slot = opposite * 2 + core
        rest_copy(0, slot, other, half).wait_recv()
        hand_on(9 + half, slot, other, half)
    for chip in (left, right):
        rest_copy(0, chip * 2 + 1 - core, other).wait_recv()
    look((left * 2 + 1 - core, right * 2 + 1 - core), False, False, 0, chunks)
    for half in range(2):
        rest_copy(0, opposite * 2 + 1 - core, other, half).wait_recv()
    look((opposite * 2 + core, opposite * 2 + 1 - core), False, True, 0, chunks)

    state = [state_ref[e : e + 1, :] for e in range(12)]
    for it in range(NEWTON):
        pick = iota((16, 128), 1) < B
        low = (fkd[...] >> 9) & 127
        chip_of = fkd[...] >> 16
        far = [None] * 12
        for n, chip in enumerate((here, right, left, opposite)):
            for k in range(2):
                if n:
                    state_copy(it, c, chip * 2 + k).wait_recv()
                elif k:
                    state_copy(it, c, other).wait_recv()
            table = jnp.where(pick, srecv[it, 2 * chip], srecv[it, 2 * chip + 1])
            mine = chip_of == chip
            for e in range(12):
                value = gather_lanes(table[e : e + 1], low)
                far[e] = value if n == 0 else jnp.where(mine, value, far[e])
        for i in range(3):
            xd[i] = far[i] + fr[0] * far[3 + i] + fr[1] * far[6 + i] + fr[2] * far[9 + i]

        for j in range(NG):
            for i in range(3):
                for t in range(3):
                    at = i * PER_G + t * 128
                    xsend[it, j, :, at : at + 128] = xd[i, j * 3 + t : j * 3 + t + 1, :]

        for d in range(1, NG):
            x_copy(it, group_peer(d), g).start()

        xrecv[it, g] = xsend[it, g]

        near_index = nb[...]
        near = [gather_lanes(jnp.concatenate([s, s], axis=1), near_index) for s in state]
        near_x = [
            near[i] + nr[0] * near[3 + i] + nr[1] * near[6 + i] + nr[2] * near[9 + i]
            for i in range(3)
        ]

        for i in range(3):
            nr4[i] = near_x[i]
        both = jnp.zeros((2 * FEATURES, B), F32)
        for part in range(0, NG, PART):
            for q in range(part, part + PART):
                if q:
                    x_copy(it, g, groups[q]).wait_recv()
                for i in range(3):
                    for t in range(3):
                        at = i * PER_G + t * 128
                        xd[i, q * 3 + t : q * 3 + t + 1, :] = xrecv[it, groups[q], :, at : at + 128]

            rows = slice(part * 3, (part + PART) * 3)
            off = [nr4[i, rows] - xd[i, rows] for i in range(3)]
            w = 1.0 / (off[0] * off[0] + off[1] * off[1] + off[2] * off[2] + 1.0)
            h1 = (2.0 * kc) * w * w * live[rows]
            h2 = 4.0 * h1 * w
            for f, (i, k) in enumerate(IK):
                value = h2 * off[i] * off[k]
                at = pl.ds(rows.start * 8 + f, PART * 3, stride=8)
                q8[at, :] = value + h1 if i == k else value
            for i in range(2):
                q8[pl.ds(rows.start * 8 + 6 + i, PART * 3, stride=8), :] = -h1 * off[i]
            q2[rows, :] = -h1 * off[2]

            for first in range(rows.start, rows.stop, 4):
                for j in range(first, first + 4):
                    lanes = pl.ds(j * 128, 128)
                    terms = q8[j * 8 : j * 8 + 8, :]
                    values = [terms * p16[f : f + 1, lanes] for f in range(10)]
                    values.append(p16[0:8, lanes] * q2[j : j + 1, :])
                    high = [value.astype(BF16) for value in values]
                    low = [(v - h.astype(F32)).astype(BF16) for v, h in zip(values, high)]
                    feat[:, lanes] = jnp.concatenate(high + low, axis=0)
                block = pl.ds(first * 128, 4 * 128)
                both = both + lax.dot_general(
                    feat[:, block], ohb[:, block], NT, preferred_element_type=F32
                )
        tot[...] = both[0:FEATURES] + both[FEATURES : 2 * FEATURES]

        def moment(m, n):
            f = MN.index((min(m, n), max(m, n)))
            return inert[f : f + 1, :]

        def hess(a, b):
            (m, i), (n, k) = divmod(a, 3), divmod(b, 3)
            f = IK.index((min(i, k), max(i, k))) + MN.index((min(m, n), max(m, n))) * 8
            value = tot[f : f + 1, :]
            if i == k:
                value = value + moment(m, n)
            if a == b and m > 0:
                value = value + 2.0 * KAPPA
            return value

        shift = [state[e] - pred_ref[e : e + 1, :] for e in range(12)]
        grad = []
        for e in range(12):
            m, i = divmod(e, 3)
            at = m * 8 + 6 + i if i < 2 else 80 + m
            value = tot[at : at + 1, :]
            for n in range(4):
                value = value + moment(m, n) * shift[3 * n + i]
            if m > 0:
                value = value + 2.0 * KAPPA * (state[e] - (1.0 if m - 1 == i else 0.0))
            grad.append(value)
        step = solve(hess, grad)
        state = [state[e] - step[e] for e in range(12)]
        if it + 1 < NEWTON:
            for e in range(12):
                ssend[it + 1, e : e + 1, :] = jnp.concatenate([state[e], state[e]], axis=1)

            for d in range(1, NC):
                state_copy(it + 1, cell_peer(d), c).start()

            srecv[it + 1, c] = ssend[it + 1]
        else:
            for e in range(12):
                out_ref[e : e + 1, :] = state[e]

    for copy in rest_sends:
        copy.wait_send()

    for d in range(1, NC):
        key_copy(cell_peer(d), c).wait_send()
        for it in range(NEWTON):
            state_copy(it, cell_peer(d), c).wait_send()

    for d in range(1, NG):
        for it in range(NEWTON):
            x_copy(it, group_peer(d), g).wait_send()


def on_device(rest, state, pred, mass, pair_body, pair_vertex, far_body, far_vertex, counts):
    dma = pltpu.SemaphoreType.DMA
    vmem = pltpu.VMEM
    return pl.pallas_call(
        kernel,
        out_shape=jax.ShapeDtypeStruct((12, B), F32),
        in_specs=[pl.BlockSpec(memory_space=pltpu.HBM)] * 9,
        out_specs=pl.BlockSpec(memory_space=vmem),
        scratch_shapes=[
            vmem((12, B), F32),
            vmem((12, B), F32),
            vmem((1, B), F32),
            vmem(DENSE, I32),
            vmem(DENSE, I32),
            vmem(DENSE, I32),
            vmem(DENSE, I32),
            vmem((1, 128), I32),
            vmem((NC, 3 * B, V), BF16),
            vmem((NC, NG, 128), I32),
            vmem((NC, NG, 128), I32),
            vmem((NEWTON, 16, 128), F32),
            vmem((NEWTON, NC, 16, 128), F32),
            vmem((NEWTON, NG, 1, 3 * PER_G), F32),
            vmem((NEWTON, NG, 1, 3 * PER_G), F32),
            vmem((V, ROWS), BF16),
            vmem((B, ROWS), BF16),
            vmem((24, ROWS), F32),
            vmem((NG, PER_G), I32),
            vmem(DENSE, I32),
            vmem((3,) + DENSE, F32),
            vmem((3,) + DENSE, F32),
            vmem((3,) + DENSE, F32),
            vmem(DENSE, I32),
            vmem(DENSE, I32),
            vmem(DENSE, F32),
            vmem((16, ROWS), F32),
            vmem((8 * DENSE[0], 128), F32),
            vmem(DENSE, F32),
            vmem((2 * FEATURES, ROWS), BF16),
            vmem((FEATURES, B), F32),
            vmem((16, B), F32),
            vmem((3,) + DENSE, F32),
            dma((9,)),
            dma((11,)),
            dma((NC, 2)),
            dma((NC,)),
            dma((NC,)),
            dma((NEWTON, NC)),
            dma((NEWTON, NC)),
            dma((NEWTON, NG)),
            dma((NEWTON, NG)),
        ],
        compiler_params=pltpu.CompilerParams(
            collective_id=0, has_side_effects=True, vmem_limit_bytes=60 * 2**20
        ),
    )(
        rest.reshape(3 * B, V),
        state,
        pred,
        mass.reshape(1, B),
        pair_body.reshape(DENSE),
        pair_vertex.reshape(DENSE),
        far_body.reshape(DENSE),
        far_vertex.reshape(DENSE),
        counts,
    )


def solution(mesh):
    both = ("group", "cell")
    return jax.shard_map(
        on_device,
        mesh=mesh,
        in_specs=(
            P(None, both, None),
            P(None, both),
            P(None, both),
            P(both),
            P(both),
            P(both),
            P(both),
            P(both),
            P(both, None),
        ),
        out_specs=P(None, both),
        check_vma=False,
    )
```

```python
import jax
import jax.numpy as jnp
from jax import lax
from jax.experimental import pallas as pl
from jax.experimental.pallas import tpu as pltpu
from jax.sharding import PartitionSpec as P

NEWTON = 2
KC0 = 40.0
KAPPA = 2.0
MESH = pl.DeviceIdType.MESH
F32 = jnp.float32
BF16 = jnp.bfloat16
I32 = jnp.int32

V = 512
B = 64
ROWS = 6144
CAP = 48
NG = 16
NC = 8
DENSE = (ROWS // 128, 128)
PER_G = ROWS // NG
W = 256
NEAREST = sorted(
    ((z, y) for z in range(4) for y in range(4)),
    key=lambda d: min(d[0], 4 - d[0]) + min(d[1], 4 - d[1]),
)
PART = 2
FEATURES = 88
NT = (((1,), (1,)), ((), ()))

MN = [(m, n) for m in range(4) for n in range(m, 4)]
IK = [(i, k) for i in range(3) for k in range(i, 3)]


def iota(shape, dim):
    return lax.broadcasted_iota(I32, shape, dim)


def one_hot_vertex(vertex):
    width = vertex.shape[1]
    rows = (iota((V, width), 0) - V // 2).astype(BF16)
    mine = jnp.broadcast_to((vertex - V // 2).astype(BF16), (V, width))
    return jnp.where(rows == mine, jnp.ones((), BF16), jnp.zeros((), BF16))


def pair_of(ref, j):
    return jnp.concatenate([ref[pl.ds(2 * j, 1), :], ref[pl.ds(2 * j + 1, 1), :]], axis=1)


def pick_bodies(acc, picked, body, blocks):
    for n in range(blocks):
        for bg in range(B // 8):
            mine = body == n * B + bg * 8
            for c in range(3):
                at = n * 3 * B + c * B + bg * 8
                acc[c] = jnp.where(mine, picked[at : at + 8], acc[c])
    return acc


def gather_lanes(row, index):
    return jnp.take_along_axis(
        jnp.broadcast_to(row, index.shape), index, axis=1, mode="promise_in_bounds"
    )


def solve(hess, grad):
    factor = [[None] * 12 for _ in range(12)]
    inv = [None] * 12
    for col in range(12):
        running = hess(col, col)
        for inner in range(col):
            running = running - factor[col][inner] * factor[col][inner]
        inv[col] = 1.0 / jnp.sqrt(running)
        for row in range(col + 1, 12):
            value = hess(row, col)
            for inner in range(col):
                value = value - factor[row][inner] * factor[col][inner]
            factor[row][col] = value * inv[col]
    forward = []
    for row in range(12):
        running = grad[row]
        for col in range(row):
            running = running - factor[row][col] * forward[col]
        forward.append(running * inv[row])
    backward = [None] * 12
    for row in reversed(range(12)):
        running = forward[row]
        for col in range(row + 1, 12):
            running = running - factor[col][row] * backward[col]
        backward[row] = running * inv[row]
    return backward


def kernel(
    rest_in, state_in, pred_in, mass_in, nb_in, nv_in, fb_in, fv_in, counts_in,
    out_ref,
    state_ref, pred_ref, mass_ref, nb_ref, nv_ref, fb_ref, fv_ref, counts_ref,
    restg, ksend, krecv, ssend, srecv, xsend, xrecv,
    oh, ohb, acc, keyd, fkd, fr, early, nr, nr4, nb, nv, live, p16, q8, q2, feat, tot, inert, xd,
    in_s, rest_ss, rest_rs, k_ss, k_rs, s_ss, s_rs, x_ss, x_rs,
):
    g = lax.axis_index("group")
    c = lax.axis_index("cell")
    kc = KC0 * B / ROWS

    def cell_peer(d):
        return lax.rem(c + d, NC)

    z, y = lax.div(g, 4), lax.rem(g, 4)
    groups = [lax.rem(z + dz, 4) * 4 + lax.rem(y + dy, 4) for dz, dy in NEAREST]

    def group_peer(d):
        return lax.rem(g + d, NG)

    to_vmem = [
        pltpu.make_async_copy(source, target, in_s.at[n])
        for n, (source, target) in enumerate(
            (
                (fb_in, fb_ref), (fv_in, fv_ref), (state_in, state_ref), (nv_in, nv_ref),
                (nb_in, nb_ref), (rest_in, restg.at[c]), (counts_in, counts_ref),
                (mass_in, mass_ref), (pred_in, pred_ref),
            )
        )
    ]
    for copy in to_vmem:
        copy.start()

    barrier = pltpu.get_barrier_semaphore()

    for d in range(1, NC):
        pl.semaphore_signal(barrier, inc=1, device_id=(g, cell_peer(d)), device_id_type=MESH)

    for d in range(1, NG):
        pl.semaphore_signal(barrier, inc=1, device_id=(group_peer(d), c), device_id_type=MESH)

    for copy in to_vmem[:3]:
        copy.wait()

    for t in range(3):
        rows = pl.ds(t, NG, stride=3)
        keyd[:, t * 128 : (t + 1) * 128] = fb_ref[rows, :] * V + fv_ref[rows, :]
    ksend[...] = jnp.zeros_like(ksend)
    for s in range(NC):
        ksend[s, :, 0:CAP] = keyd[:, s * CAP : (s + 1) * CAP]
    ssend[...] = jnp.zeros_like(ssend)
    ssend[0, 0:12, :] = jnp.concatenate([state_ref[...], state_ref[...]], axis=1)

    pl.semaphore_wait(barrier, NC - 1 + NG - 1)

    def key_copy(to, slot):
        return pltpu.make_async_remote_copy(
            ksend.at[to], krecv.at[slot], k_ss.at[to], k_rs.at[slot],
            device_id=(g, to), device_id_type=MESH,
        )

    x, core = lax.div(c, 2), lax.rem(c, 2)
    chips = [lax.rem(x + d, NC // 2) for d in range(NC // 2)]
    here, right, opposite, left = chips
    other = here * 2 + 1 - core
    halves = (pl.ds(0, 3 * B // 2), pl.ds(3 * B // 2, 3 * B // 2))

    def rest_copy(n, slot, to, half=None):
        ref = restg.at[slot] if half is None else restg.at[slot, halves[half]]
        return pltpu.make_async_remote_copy(
            ref, ref, rest_ss.at[n], rest_rs.at[slot, half or 0],
            device_id=(g, to), device_id_type=MESH,
        )

    def first_copy(n, to, half=None):
        source = rest_in if half is None else rest_in.at[halves[half]]
        target = restg.at[c] if half is None else restg.at[c, halves[half]]
        return pltpu.make_async_remote_copy(
            source, target, rest_ss.at[n], rest_rs.at[c, half or 0],
            device_id=(g, to), device_id_type=MESH,
        )

    rest_sends = [
        first_copy(0, right * 2 + core, 0),
        first_copy(1, left * 2 + core, 1),
        first_copy(2, other),
        first_copy(3, right * 2 + core, 1),
        first_copy(4, left * 2 + core, 0),
    ]

    def hand_on(n, slot, to, half=None):
        copy = rest_copy(n, slot, to, half)
        copy.start()
        rest_sends.append(copy)

    def state_copy(it, to, slot):
        return pltpu.make_async_remote_copy(
            ssend.at[it], srecv.at[it, slot], s_ss.at[it, to], s_rs.at[it, slot],
            device_id=(g, to), device_id_type=MESH,
        )

    def x_copy(it, to, slot):
        return pltpu.make_async_remote_copy(
            xsend.at[it, to], xrecv.at[it, slot], x_ss.at[it, to], x_rs.at[it, slot],
            device_id=(to, c), device_id_type=MESH,
        )

    for d in range(1, NC):
        key_copy(cell_peer(d), c).start()

    for copy in rest_sends:
        copy.start()

    for d in range(1, NC):
        state_copy(0, cell_peer(d), c).start()

    krecv[c] = ksend[c]
    srecv[0, c] = ssend[0]
    for copy in to_vmem[3:]:
        copy.wait()

    row = iota(DENSE, 0) * 128 + iota(DENSE, 1)
    sender = (row * 43691) >> 21
    count = gather_lanes(counts_ref[...], sender)
    xd[0] = jnp.where(row - sender * CAP < count, 1.0, 0.0)

    for q, group in enumerate(groups):
        for t in range(3):
            at = pl.ds(group * 3 + t, 1)
            to = pl.ds(q * 3 + t, 1)
            nb[to, :] = nb_ref[at, :]
            nv[to, :] = nv_ref[at, :]
            live[to, :] = xd[0, at, :]

    p16[...] = jnp.zeros_like(p16)

    def near_lookup(j, carry):
        lanes = pl.ds(pl.multiple_of(j * W, W), W)
        picked = jnp.dot(restg[c], one_hot_vertex(pair_of(nv, j)), preferred_element_type=F32)
        body = pair_of(nb, j)
        ohb[:, lanes] = jnp.where(
            iota((B, W), 0) == jnp.broadcast_to(body, (B, W)), 1.0, 0.0
        ).astype(BF16)
        tile = jnp.broadcast_to(body, (8, W)) - iota((8, W), 0)
        found = pick_bodies([jnp.zeros((8, W), F32)] * 3, picked, tile, 1)
        r = [jnp.sum(f, 0, keepdims=True) for f in found]
        lever = [jnp.ones((1, W), F32)] + r
        for f, (m, n) in enumerate(MN):
            p16[f : f + 1, lanes] = lever[m] * lever[n]
        for i in range(3):
            for t in range(2):
                nr[i, pl.ds(2 * j + t, 1), :] = r[i][:, t * 128 : (t + 1) * 128]
        return carry

    lax.fori_loop(0, ROWS // W, near_lookup, 0, unroll=4)

    ones = jnp.ones((8, V), BF16)
    body_rest = [restg[c, i * B : (i + 1) * B, :] for i in range(3)]
    scale = mass_ref[...] * (1.0 / V)
    inert[0:1, :] = mass_ref[...]
    for f, (m, n) in enumerate(MN):
        if n == 0:
            continue
        if m == 0:
            total = lax.dot_general(ones, body_rest[n - 1], NT, preferred_element_type=F32)
        else:
            product = body_rest[m - 1].astype(F32) * body_rest[n - 1].astype(F32)
            high = product.astype(BF16)
            low = (product - high.astype(F32)).astype(BF16)
            total = lax.dot_general(ones, high, NT, preferred_element_type=F32)
            total = total + lax.dot_general(ones, low, NT, preferred_element_type=F32)
        inert[f : f + 1, :] = total[0:1] * scale

    for d in range(1, NC):
        key_copy(c, cell_peer(d)).wait_recv()

    for s in range(NC):
        keyd[:, s * CAP : (s + 1) * CAP] = krecv[s, :, 0:CAP]
    for t in range(3):
        fkd[pl.ds(t, NG, stride=3), :] = keyd[:, t * 128 : (t + 1) * 128]

    def far_states(it):
        pick = iota((16, 128), 1) < B
        low = (fkd[...] >> 9) & 127
        chip_of = fkd[...] >> 16
        far = [None] * 12
        for n, chip in enumerate((here, right, left, opposite)):
            for k in range(2):
                if n:
                    state_copy(it, c, chip * 2 + k).wait_recv()
                elif k:
                    state_copy(it, c, other).wait_recv()
            table = jnp.where(pick, srecv[it, 2 * chip], srecv[it, 2 * chip + 1])
            mine = chip_of == chip
            for e in range(12):
                value = gather_lanes(table[e : e + 1], low)
                far[e] = value if n == 0 else jnp.where(mine, value, far[e])
        return far

    def look(where, first, last, start, stop):
        def step(j, carry):
            lanes = pl.ds(pl.multiple_of(j * W, W), W)
            key = pair_of(fkd, j)
            if first:
                hot = one_hot_vertex(key & (V - 1))
                oh[:, lanes] = hot
                found = [jnp.zeros((8, W), F32)] * 3
            else:
                hot = oh[:, lanes]
                found = [acc[i * 8 : i * 8 + 8, lanes] for i in range(3)]
            body = jnp.broadcast_to(key >> 9, (8, W)) - iota((8, W), 0)
            for slot in where:
                picked = jnp.dot(restg[slot], hot, preferred_element_type=F32)
                found = pick_bodies(found, picked, body - slot * B, 1)
            for i in range(3):
                if last:
                    r = jnp.sum(found[i], 0, keepdims=True)
                    for t in range(2):
                        fr[i, pl.ds(2 * j + t, 1), :] = r[:, t * 128 : (t + 1) * 128]
                else:
                    acc[i * 8 : i * 8 + 8, lanes] = found[i]
            return carry

        lax.fori_loop(start, stop, step, 0, unroll=True)

    chunks = ROWS // W
    rest_copy(0, other, other).wait_recv()
    look((c, other), True, False, 0, 10)
    for n, (chip, half, to) in enumerate(((left, 0, right), (right, 1, left))):
        rest_copy(0, chip * 2 + core, other, half).wait_recv()
        hand_on(5 + n, chip * 2 + core, to * 2 + core, half)
    look((c, other), True, False, 10, 24)
    for n, (chip, half) in enumerate(((left, 1), (right, 0))):
        rest_copy(0, chip * 2 + core, other, half).wait_recv()
        hand_on(7 + n, chip * 2 + core, other)
    look((left * 2 + core, right * 2 + core), False, False, 0, 24)
    for half in range(2):
        slot = opposite * 2 + core
        rest_copy(0, slot, other, half).wait_recv()
        hand_on(9 + half, slot, other, half)
    for chip in (left, right):
        rest_copy(0, chip * 2 + 1 - core, other).wait_recv()
    look((left * 2 + 1 - core, right * 2 + 1 - core), False, False, 0, chunks)
    for e, value in enumerate(far_states(0)):
        early[e] = value
    for half in range(2):
        rest_copy(0, opposite * 2 + 1 - core, other, half).wait_recv()
    look((opposite * 2 + core, opposite * 2 + 1 - core), False, True, 0, chunks)

    state = [state_ref[e : e + 1, :] for e in range(12)]
    for it in range(NEWTON):
        far = early if it == 0 else far_states(it)
        for i in range(3):
            xd[i] = far[i] + fr[0] * far[3 + i] + fr[1] * far[6 + i] + fr[2] * far[9 + i]

        for j in range(NG):
            for i in range(3):
                for t in range(3):
                    at = i * PER_G + t * 128
                    xsend[it, j, :, at : at + 128] = xd[i, j * 3 + t : j * 3 + t + 1, :]

        for d in range(1, NG):
            x_copy(it, group_peer(d), g).start()

        xrecv[it, g] = xsend[it, g]

        near_index = nb[...]
        near = [gather_lanes(jnp.concatenate([s, s], axis=1), near_index) for s in state]
        near_x = [
            near[i] + nr[0] * near[3 + i] + nr[1] * near[6 + i] + nr[2] * near[9 + i]
            for i in range(3)
        ]

        for i in range(3):
            nr4[i] = near_x[i]
        if it + 1 == NEWTON:
            for copy in rest_sends:
                copy.wait_send()
            for d in range(1, NC):
                key_copy(cell_peer(d), c).wait_send()
                for n in range(NEWTON):
                    state_copy(n, cell_peer(d), c).wait_send()
            for n in range(NEWTON):
                for d in range(1, NG):
                    x_copy(n, group_peer(d), g).wait_send()

        both = jnp.zeros((2 * FEATURES, B), F32)
        for part in range(0, NG, PART):
            for q in range(part, part + PART):
                if q:
                    x_copy(it, g, groups[q]).wait_recv()
                for i in range(3):
                    for t in range(3):
                        at = i * PER_G + t * 128
                        xd[i, q * 3 + t : q * 3 + t + 1, :] = xrecv[it, groups[q], :, at : at + 128]

            rows = slice(part * 3, (part + PART) * 3)
            off = [nr4[i, rows] - xd[i, rows] for i in range(3)]
            w = 1.0 / (off[0] * off[0] + off[1] * off[1] + off[2] * off[2] + 1.0)
            h1 = (2.0 * kc) * w * w * live[rows]
            h2 = 4.0 * h1 * w
            for f, (i, k) in enumerate(IK):
                value = h2 * off[i] * off[k]
                at = pl.ds(rows.start * 8 + f, PART * 3, stride=8)
                q8[at, :] = value + h1 if i == k else value
            for i in range(2):
                q8[pl.ds(rows.start * 8 + 6 + i, PART * 3, stride=8), :] = -h1 * off[i]
            q2[rows, :] = -h1 * off[2]

            for first in range(rows.start, rows.stop, 6):
                for j in range(first, first + 6):
                    lanes = pl.ds(j * 128, 128)
                    terms = q8[j * 8 : j * 8 + 8, :]
                    values = [terms * p16[f : f + 1, lanes] for f in range(10)]
                    values.append(p16[0:8, lanes] * q2[j : j + 1, :])
                    high = [value.astype(BF16) for value in values]
                    low = [(v - h.astype(F32)).astype(BF16) for v, h in zip(values, high)]
                    feat[:, lanes] = jnp.concatenate(high + low, axis=0)
                block = pl.ds(first * 128, 6 * 128)
                both = both + lax.dot_general(
                    feat[:, block], ohb[:, block], NT, preferred_element_type=F32
                )
        tot[...] = both[0:FEATURES] + both[FEATURES : 2 * FEATURES]

        def moment(m, n):
            f = MN.index((min(m, n), max(m, n)))
            return inert[f : f + 1, :]

        def hess(a, b):
            (m, i), (n, k) = divmod(a, 3), divmod(b, 3)
            f = IK.index((min(i, k), max(i, k))) + MN.index((min(m, n), max(m, n))) * 8
            value = tot[f : f + 1, :]
            if i == k:
                value = value + moment(m, n)
            if a == b and m > 0:
                value = value + 2.0 * KAPPA
            return value

        shift = [state[e] - pred_ref[e : e + 1, :] for e in range(12)]
        grad = []
        for e in range(12):
            m, i = divmod(e, 3)
            at = m * 8 + 6 + i if i < 2 else 80 + m
            value = tot[at : at + 1, :]
            for n in range(4):
                value = value + moment(m, n) * shift[3 * n + i]
            if m > 0:
                value = value + 2.0 * KAPPA * (state[e] - (1.0 if m - 1 == i else 0.0))
            grad.append(value)
        step = solve(hess, grad)
        state = [state[e] - step[e] for e in range(12)]
        if it + 1 < NEWTON:
            for e in range(12):
                ssend[it + 1, e : e + 1, :] = jnp.concatenate([state[e], state[e]], axis=1)

            for d in range(1, NC):
                state_copy(it + 1, cell_peer(d), c).start()

            srecv[it + 1, c] = ssend[it + 1]
        else:
            for e in range(12):
                out_ref[e : e + 1, :] = state[e]


def on_device(rest, state, pred, mass, pair_body, pair_vertex, far_body, far_vertex, counts):
    dma = pltpu.SemaphoreType.DMA
    vmem = pltpu.VMEM
    return pl.pallas_call(
        kernel,
        out_shape=jax.ShapeDtypeStruct((12, B), F32),
        in_specs=[pl.BlockSpec(memory_space=pltpu.HBM)] * 9,
        out_specs=pl.BlockSpec(memory_space=vmem),
        scratch_shapes=[
            vmem((12, B), F32),
            vmem((12, B), F32),
            vmem((1, B), F32),
            vmem(DENSE, I32),
            vmem(DENSE, I32),
            vmem(DENSE, I32),
            vmem(DENSE, I32),
            vmem((1, 128), I32),
            vmem((NC, 3 * B, V), BF16),
            vmem((NC, NG, 128), I32),
            vmem((NC, NG, 128), I32),
            vmem((NEWTON, 16, 128), F32),
            vmem((NEWTON, NC, 16, 128), F32),
            vmem((NEWTON, NG, 1, 3 * PER_G), F32),
            vmem((NEWTON, NG, 1, 3 * PER_G), F32),
            vmem((V, ROWS), BF16),
            vmem((B, ROWS), BF16),
            vmem((24, ROWS), F32),
            vmem((NG, PER_G), I32),
            vmem(DENSE, I32),
            vmem((3,) + DENSE, F32),
            vmem((12,) + DENSE, F32),
            vmem((3,) + DENSE, F32),
            vmem((3,) + DENSE, F32),
            vmem(DENSE, I32),
            vmem(DENSE, I32),
            vmem(DENSE, F32),
            vmem((16, ROWS), F32),
            vmem((8 * DENSE[0], 128), F32),
            vmem(DENSE, F32),
            vmem((2 * FEATURES, ROWS), BF16),
            vmem((FEATURES, B), F32),
            vmem((16, B), F32),
            vmem((3,) + DENSE, F32),
            dma((9,)),
            dma((11,)),
            dma((NC, 2)),
            dma((NC,)),
            dma((NC,)),
            dma((NEWTON, NC)),
            dma((NEWTON, NC)),
            dma((NEWTON, NG)),
            dma((NEWTON, NG)),
        ],
        compiler_params=pltpu.CompilerParams(
            collective_id=0, has_side_effects=True, vmem_limit_bytes=60 * 2**20
        ),
    )(
        rest.reshape(3 * B, V),
        state,
        pred,
        mass.reshape(1, B),
        pair_body.reshape(DENSE),
        pair_vertex.reshape(DENSE),
        far_body.reshape(DENSE),
        far_vertex.reshape(DENSE),
        counts,
    )


def solution(mesh):
    both = ("group", "cell")
    return jax.shard_map(
        on_device,
        mesh=mesh,
        in_specs=(
            P(None, both, None),
            P(None, both),
            P(None, both),
            P(both),
            P(both),
            P(both),
            P(both),
            P(both),
            P(both, None),
        ),
        out_specs=P(None, both),
        check_vma=False,
    )
```
